128 devices in a mesh: dp: 4 (over y_lo, core), expert: 32 (over z, x, y_hi).
Axes of the slice: x: 4, y: 4 (y_hi: 2, y_lo: 2; y = y_hi * 2 + y_lo), z: 4, core: 2. Of those that a mesh axis runs over, the one named last changes fastest.
Arguments:
- inputs: bfloat16 [262144, 1024], P(('dp', 'expert')), may hold values from -6 to 6
- cotangent: bfloat16 [262144, 1024], P(('dp', 'expert')), may hold values from -6 to 6
- expert_weights: bfloat16 [32, 2, 512, 512], P('expert'), may hold values from -1 to 1
- fidelity_table: float32 [4, 32], replicated, may hold values from 0.009375 to 0.09375
- system_weights: float32 [8, 32], P('dp'), may hold values from 0.3 to 3
- fidelity: int32 [8], P('dp'), may hold values from 0 to 3
- block_system: int32 [2048], P(('dp', 'expert')), may hold values from 0 to 1
- block_count: int32 [2048], P(('dp', 'expert')), may hold values from 1 to 128, 196608 in all
Outputs:
- messages: bfloat16 [262144, 1024], P(('dp', 'expert'))
- grad_inputs: bfloat16 [262144, 1024], P(('dp', 'expert'))
- grad_experts: float32 [32, 2, 512, 512], P('expert')
The draws below stay inside these ranges and needn't reach their ends.
All inputs are finite; a program needn't handle non-finite values. No bound on the sum of `block_count` on one device may be relied on, other than what follows from the above.
Results may differ from the reference program's by a relative error of at most 0.0049.
Values may be sent and summed in bfloat16 or wider, within the bound.
No kernel may reach another device: no remote copies, remote signals or barrier semaphores. Data moves between devices by JAX's collectives and lax.ppermute only.
A program may use at most 128 MiB of HBM per device.

```python
import math
import jax
import jax.numpy as jnp
import numpy as np
from jax import lax

C = 512
FIDS = 4
BLOCK = 128
SYS_GRP = 2
EXPERTS = 32
SYSTEMS = 8
BLOCKS = 2048
EDGES = 262144
N_DP = 4


def with_ends(array, own_key, least, high):
    extent = array.shape
    spot = [jax.random.randint(jax.random.fold_in(own_key, axis), (), 0, extent[axis]) for axis in range(len(extent))]
    array = array.at[tuple(spot)].set(least)
    longest = extent.index(max(extent))
    spot[longest] = (spot[longest] + 1) % extent[longest]
    return array.at[tuple(spot)].set(high)


def levels(rng, extent, cuts, least, top_value):
    def one(dim, parts):
        heights = jax.random.uniform(jax.random.fold_in(jax.random.fold_in(rng, 6), dim), (parts,), jnp.float32, least / len(cuts), top_value / len(cuts))
        return jnp.repeat(jnp.exp(heights), extent[dim] // parts).reshape((-1,) + (1,) * (len(extent) - dim - 1))

    level = one(*cuts[0])
    for cut in cuts[1:]:
        level = level * one(*cut)
    return level


def split_up(count, total, reach, skew):
    portions = [(1 << 20) // math.isqrt(rank ** skew) + 1 for rank in range(2, count + 1)]
    rest, counts = total - reach - (count - 1), [1] * (count - 1)
    while rest > 0:
        free = [i for i in range(count - 1) if counts[i] < reach]
        mass, budget = sum([portions[i] for i in free]), rest
        for i in free:
            addition = min(reach - counts[i], max(1, budget * portions[i] // mass), rest)
            counts[i] = counts[i] + addition
            rest = rest - addition
    return np.array([reach] + counts)


def uneven(stream_key, amount, total, most, slope):
    if amount == 2:
        one = jax.random.randint(stream_key, (), max(1, total - most), min(most, total - 1) + 1)
        return jnp.stack([one, total - one])
    sizes = jnp.asarray(split_up(amount, total, most, slope), jnp.int32)
    couples = (amount - 1) // 2
    source_of, taker = sizes[1:1 + 2 * couples:2], sizes[2:2 + 2 * couples:2]
    margin = jnp.minimum(source_of - 1, most - taker)
    moved = jax.random.randint(jax.random.fold_in(stream_key, 1), (couples,), 0, 1 << 20) % (margin + 1)
    sizes = sizes.at[1:1 + 2 * couples:2].set(source_of - moved).at[2:2 + 2 * couples:2].set(taker + moved)
    return sizes[jax.random.permutation(jax.random.fold_in(stream_key, 2), amount)]


def scatter_about(stream_key, shape, spread, most, split=(), held_as=jnp.bfloat16):
    array = jax.random.normal(stream_key, shape, jnp.float32) * spread
    if len(split) > 0:
        array = levels(stream_key, shape, split, -0.22, 0.18) * array
    return jnp.clip(array, min=-most, max=most).astype(held_as)


def setup_inputs(seed: int = 0) -> dict:
    key_list = jax.random.split(jax.random.key(seed), 9)
    inputs = scatter_about(key_list[0], (EDGES, 2 * C), 1.0, 6.0, ((0, 128),))
    cotangent = scatter_about(key_list[1], (EDGES, 2 * C), 1.0, 6.0, ((0, 128),))
    expert_weights = scatter_about(key_list[2], (EXPERTS, 2, C, C), (2 * C // EXPERTS) ** -0.5, 1.0, ((0, 32),))
    fidelity_table = jnp.clip(jnp.exp(jax.random.uniform(key_list[3], (FIDS, EXPERTS), jnp.float32, math.log(0.009375), math.log(0.09375))), 0.009375, 0.09375)
    system_weights = jnp.clip(jnp.exp(math.log(3.0) - 2.3025851 * jax.random.uniform(key_list[4], (SYSTEMS, EXPERTS), jnp.float32) ** levels(key_list[4], (SYSTEMS, EXPERTS), ((0, 4),), -0.2, 0.2)), 0.3, 3.0)
    fidelity = with_ends(jax.random.randint(key_list[5], (SYSTEMS,), 0, FIDS), jax.random.fold_in(key_list[5], 1), 0, FIDS - 1).astype(jnp.int32)
    block_system = with_ends(jax.random.randint(key_list[6], (BLOCKS,), 0, SYS_GRP), jax.random.fold_in(key_list[6], 1), 0, SYS_GRP - 1).astype(jnp.int32)
    block_count = uneven(key_list[7], BLOCKS, BLOCKS * 96, BLOCK, 1).astype(jnp.int32)
    return dict(inputs=inputs, cotangent=cotangent, expert_weights=expert_weights, fidelity_table=fidelity_table, system_weights=system_weights, fidelity=fidelity, block_system=block_system, block_count=block_count)


def mix_weights(fidelity, system_weights, fidelity_table):
    onehot = (fidelity[:, None] == jnp.arange(FIDS, dtype=jnp.int32)[None, :]).astype(jnp.float32)
    return jnp.dot(onehot, fidelity_table, precision=lax.Precision.HIGHEST) * system_weights

def widen(merged):
    real_part = merged[:, 0]
    imag_part = merged[:, 1]
    upper = jnp.concatenate([real_part, imag_part], axis=2)
    lower = jnp.concatenate([-imag_part, real_part], axis=2)
    return jnp.concatenate([upper, lower], axis=1)

def fold_square(square, width):
    real_grad = square[:, :width, :width] + square[:, width:, width:]
    imag_grad = square[:, :width, width:] - square[:, width:, :width]
    return jnp.stack([real_grad, imag_grad], axis=1)

def block_pass(wide, grads, features, upstream, system, count):
    weight = wide[system]
    valid = (jnp.arange(features.shape[0], dtype=jnp.int32) < count)[:, None]
    masked = jnp.where(valid, features, jnp.zeros_like(features))
    output = jnp.dot(masked, weight, preferred_element_type=jnp.float32).astype(jnp.bfloat16)
    back = lax.dot_general(upstream, weight, (((1,), (1,)), ((), ())), preferred_element_type=jnp.float32)
    back = jnp.where(valid, back, jnp.zeros_like(back)).astype(jnp.bfloat16)
    square = lax.dot_general(masked, upstream, (((0,), (0,)), ((), ())), preferred_element_type=jnp.float32)
    grads = grads.at[system].add(square)
    return (grads, output, back)

def reference(inputs, cotangent, expert_weights, fidelity_table, system_weights, fidelity, block_system, block_count):
    mixing = mix_weights(fidelity, system_weights, fidelity_table)
    merged = jnp.einsum('se,epij->spij', mixing, expert_weights.astype(jnp.float32), precision=lax.Precision.HIGHEST).astype(jnp.bfloat16)
    wide = widen(merged)
    per_group = BLOCKS // N_DP
    owners = (block_system + jnp.arange(BLOCKS, dtype=jnp.int32) // per_group * SYS_GRP).astype(jnp.int32)
    features = inputs.reshape(BLOCKS, BLOCK, 2 * C)
    upstream = cotangent.reshape(BLOCKS, BLOCK, 2 * C)

    def step(grads, items):
        feature, upward, system, count = items
        grads, output, back = block_pass(wide, grads, feature, upward, system, count)
        return (grads, (output, back))
    start = jnp.zeros((SYSTEMS, 2 * C, 2 * C), jnp.float32)
    grads, (outputs, backs) = lax.scan(step, start, (features, upstream, owners, block_count))
    grad_system = fold_square(grads, C)
    factor = EXPERTS / math.sqrt(EDGES)
    grad_experts = jnp.einsum('se,spij->epij', mixing, grad_system, precision=lax.Precision.HIGHEST) * factor
    return (outputs.reshape(EDGES, 2 * C), backs.reshape(EDGES, 2 * C), grad_experts)
```

```python
import functools
import math

import jax
import jax.numpy as jnp
from jax import lax
from jax.experimental import pallas as pl
from jax.experimental.pallas import tpu as pltpu
from jax.sharding import PartitionSpec as P

BLOCK = 128
LANES = 128
TILE_ROWS = 16
GROUP = 2
VMEM_LIMIT = 56 * 1024 * 1024


def live_mask(slot_count, first_slot):
    row = lax.broadcasted_iota(jnp.int32, (BLOCK, 1), 0)
    parts = [(row < slot_count[first_slot + i]).astype(jnp.float32) for i in range(GROUP)]
    return jnp.concatenate(parts, axis=0).astype(jnp.bfloat16)


def place_blocks(blocks, system_ref, count_ref, slot_count, slot_block, start):
    def tally(b, total):
        return total + (system_ref[b] == 0).astype(jnp.int32)

    first = lax.fori_loop(0, blocks, tally, jnp.int32(0))
    groups_first = (first + GROUP - 1) // GROUP
    groups = groups_first + (blocks - first + GROUP - 1) // GROUP

    def clear(slot, _):
        slot_count[slot] = 0
        return 0

    lax.fori_loop(0, slot_count.shape[0], clear, 0)
    for system in range(2):

        def give(b, slot):
            mine = system_ref[b] == system

            @pl.when(mine)
            def _():
                slot_count[slot] = count_ref[b]
                slot_block[slot] = b
                start(b, slot)

            return slot + mine.astype(jnp.int32)

        lax.fori_loop(0, blocks, give, jnp.int32(0) if system == 0 else groups_first * GROUP)
    return groups_first, groups


def rows_of(index, size):
    return pl.ds(pl.multiple_of(index * size, size), size)


def copy_in(source, held, sems, which, block, slot):
    return pltpu.make_async_copy(
        source.at[rows_of(block, BLOCK), :], held.at[rows_of(slot, BLOCK), :], sems.at[which, slot]
    )


def await_group(group, slot_count, x_hbm, g_hbm, x_held, g_held, sems):
    for i in range(GROUP):
        slot = group * GROUP + i

        @pl.when(slot_count[slot] > 0)
        def _():
            copy_in(x_hbm, x_held, sems, 0, 0, slot).wait()
            copy_in(g_hbm, g_held, sems, 1, 0, slot).wait()

        @pl.when(slot_count[slot] == 0)
        def _():
            x_held[rows_of(slot, BLOCK), :] = jnp.zeros((BLOCK, x_held.shape[1]), x_held.dtype)
            g_held[rows_of(slot, BLOCK), :] = jnp.zeros((BLOCK, g_held.shape[1]), g_held.dtype)


def grad_kernel(
    system_ref, count_ref, group_ref, x_hbm, g_hbm, w_ref, out_ref,
    x_held, g_held, total, slot_count, slot_block, sems,
):
    blocks = x_hbm.shape[0] // BLOCK
    width = x_hbm.shape[1] // 2

    def start(b, slot):
        copy_in(x_hbm, x_held, sems, 0, b, slot).start()
        copy_in(g_hbm, g_held, sems, 1, b, slot).start()

    groups_first, groups = place_blocks(blocks, system_ref, count_ref, slot_count, slot_block, start)
    total[...] = jnp.zeros_like(total)
    own = group_ref[0]
    for half in range(2):
        pick = None
        for part in range(4):
            column = 256 * half + LANES * (part // 2)
            piece = w_ref[:, column:column + LANES].astype(jnp.float32).reshape(64, TILE_ROWS, LANES)
            piece = piece[:, 8 * (part % 2):8 * (part % 2) + 8, :]
            pick = piece if pick is None else jnp.where(own == part, piece, pick)
        out_ref[:, half, 64:72, :] = pick.astype(jnp.bfloat16)

    def step(group, _):
        await_group(group, slot_count, x_hbm, g_hbm, x_held, g_held, sems)
        rows = rows_of(group, GROUP * BLOCK)
        mask = live_mask(slot_count, group * GROUP)
        x_real = x_held[rows, :width] * mask
        x_imag = x_held[rows, width:] * mask
        g_real = g_held[rows, :width]
        g_imag = g_held[rows, width:]
        left = jnp.concatenate([x_real, x_imag], axis=0)
        right = jnp.concatenate(
            [jnp.concatenate([g_real, g_imag], axis=0), jnp.concatenate([g_imag, -g_real], axis=0)], axis=1
        )
        system = (group >= groups_first).astype(jnp.int32)
        total[system] += lax.dot_general(
            left, right, (((0,), (0,)), ((), ())), preferred_element_type=jnp.float32
        )
        return 0

    lax.fori_loop(0, groups, step, 0)
    for system in range(2):
        for plane in range(2):
            for half in range(2):
                for block in range(2):
                    column = plane * width + 256 * half + LANES * block
                    piece = total[system, :, column:column + LANES].astype(jnp.bfloat16)
                    row = system * 32 + block * TILE_ROWS
                    out_ref[plane * 32:plane * 32 + 32, half, row:row + TILE_ROWS, :] = piece.reshape(
                        32, TILE_ROWS, LANES
                    )


def mix_kernel(factor, group_ref, mix0, mix1, mix2, mix3, in_ref, out_ref, mixing):
    own = group_ref[0]
    experts = mix0.shape[1]
    for j, part in enumerate((mix0, mix1, mix2, mix3)):
        at = (own ^ j) * 2

        def spread(e, _):
            mixing[at, e] = part[0, e]
            mixing[at + 1, e] = part[1, e]
            return 0

        lax.fori_loop(0, experts, spread, 0)

    def merge(e, totals):
        pieces = [in_ref[d * experts + e, 64:72, :].astype(jnp.float32) for d in range(4)]
        return tuple(totals[s * 4 + d] + mixing[s, e] * pieces[d] for s in range(8) for d in range(4))

    zero = jnp.zeros((8, LANES), jnp.float32)
    merged = lax.fori_loop(0, experts, merge, (zero,) * 32)
    packed = [
        jnp.concatenate([merged[(2 * d + s) * 4 + i] for s in range(2) for i in range(4)], axis=0).astype(jnp.bfloat16)
        for d in range(4)
    ]

    def spread_merged(e, _):
        for d in range(4):
            out_ref[d * experts + e, 0:64, :] = packed[d]
        return 0

    lax.fori_loop(0, experts, spread_merged, 0)

    def gather(e, totals):
        return tuple(totals[d] + in_ref[d * experts + e, 0:64, :].astype(jnp.float32) for d in range(4))

    zero = jnp.zeros((64, LANES), jnp.float32)
    grads = lax.fori_loop(0, experts, gather, (zero,) * 4)

    def combine(e, _):
        result = zero[:32]
        for d in range(4):
            for s in range(2):
                result = result + (mixing[2 * d + s, e] * factor) * grads[d][32 * s:32 * s + 32]
        result = result.astype(jnp.bfloat16)
        for d in range(4):
            out_ref[d * experts + e, 64:96, :] = result
        return 0

    lax.fori_loop(0, experts, combine, 0)


def message_kernel(
    system_ref, count_ref, x_hbm, g_hbm, in_ref, out_hbm, back_hbm, expert_ref,
    x_held, g_held, out_held, back_held, wide, slot_count, slot_block, sems, out_sems,
):
    blocks = x_hbm.shape[0] // BLOCK
    width = x_hbm.shape[1] // 2

    def start(b, slot):
        copy_in(x_hbm, x_held, sems, 0, b, slot).start()
        copy_in(g_hbm, g_held, sems, 1, b, slot).start()

    groups_first, groups = place_blocks(blocks, system_ref, count_ref, slot_count, slot_block, start)
    for half in range(2):
        for block in range(2):
            column = 256 * half + LANES * block
            for system in range(2):
                row = system * 32 + block * TILE_ROWS
                piece = in_ref[:, half, row:row + TILE_ROWS, :].reshape(2 * width, LANES)
                real, imag = piece[:width], piece[width:]
                wide[system, :width, column:column + LANES] = real
                wide[system, width:, width + column:width + column + LANES] = real
                wide[system, :width, width + column:width + column + LANES] = imag
                wide[system, width:, column:column + LANES] = -imag
            row = 64 + block * TILE_ROWS
            expert_ref[:, column:column + LANES] = (
                in_ref[:, half, row:row + TILE_ROWS, :].reshape(2 * width, LANES).astype(jnp.float32)
            )

    def copies_out(slot, block):
        for which, (held, target) in enumerate(((out_held, out_hbm), (back_held, back_hbm))):
            yield pltpu.make_async_copy(
                held.at[rows_of(slot, BLOCK), :], target.at[rows_of(block, BLOCK), :], out_sems.at[which, slot]
            )

    def step(group, _):
        await_group(group, slot_count, x_hbm, g_hbm, x_held, g_held, sems)
        rows = rows_of(group, GROUP * BLOCK)
        mask = live_mask(slot_count, group * GROUP)
        system = (group >= groups_first).astype(jnp.int32)
        weight = wide[system]
        out_held[rows, :] = jnp.dot(
            x_held[rows, :] * mask, weight, preferred_element_type=jnp.float32
        ).astype(jnp.bfloat16)
        back_held[rows, :] = lax.dot_general(
            g_held[rows, :] * mask, weight, (((1,), (1,)), ((), ())), preferred_element_type=jnp.float32
        ).astype(jnp.bfloat16)
        for i in range(GROUP):
            slot = group * GROUP + i

            @pl.when(slot_count[slot] > 0)
            def _():
                for copy in copies_out(slot, slot_block[slot]):
                    copy.start()

        return 0

    lax.fori_loop(0, groups, step, 0)

    def finish(slot, _):
        @pl.when(slot_count[slot] > 0)
        def _():
            for copy in copies_out(slot, 0):
                copy.wait()

        return 0

    lax.fori_loop(0, slot_count.shape[0], finish, 0)


def local(
    inputs, cotangent, expert_weights, fidelity_table, system_weights, fidelity, block_system, block_count
):
    edges, channels = inputs.shape
    width = channels // 2
    blocks = block_system.shape[0]
    slots = blocks + GROUP * 2
    axes = ("dp", "expert")
    devices = lax.axis_size("dp") * lax.axis_size("expert")
    experts = fidelity_table.shape[1]
    own = lax.axis_index("dp").astype(jnp.int32).reshape(1)

    picked = jnp.zeros(system_weights.shape, jnp.float32)
    for f in range(fidelity_table.shape[0]):
        picked = jnp.where((fidelity == f)[:, None], fidelity_table[f][None, :], picked)
    mixing = picked * system_weights
    mixings = [mixing] + [
        lax.ppermute(mixing, "dp", [(i, i ^ j) for i in range(4)]) for j in range(1, 4)
    ]

    smem = pl.BlockSpec(memory_space=pltpu.SMEM)
    vmem = pl.BlockSpec(memory_space=pltpu.VMEM)
    hbm = pl.BlockSpec(memory_space=pl.ANY)
    params = pltpu.CompilerParams(vmem_limit_bytes=VMEM_LIMIT)
    held = pltpu.VMEM((slots * BLOCK, channels), jnp.bfloat16)
    macs = edges * channels * channels
    partial = pl.pallas_call(
        grad_kernel,
        out_shape=jax.ShapeDtypeStruct((64, 2, 72, LANES), jnp.bfloat16),
        in_specs=[smem, smem, smem, hbm, hbm, vmem],
        out_specs=vmem,
        scratch_shapes=[
            held,
            held,
            pltpu.VMEM((2, width, channels), jnp.float32),
            pltpu.SMEM((slots,), jnp.int32),
            pltpu.SMEM((slots,), jnp.int32),
            pltpu.SemaphoreType.DMA((2, slots)),
        ],
        compiler_params=params,
        cost_estimate=pl.CostEstimate(flops=2 * macs, bytes_accessed=12 * 2**20, transcendentals=0),
        name="weight_gradients",
    )(block_system, block_count, own, inputs, cotangent, expert_weights.reshape(channels, width))

    first = lax.all_to_all(
        partial.reshape(devices, 72, LANES), axes, split_axis=0, concat_axis=0, tiled=True
    )
    factor = experts / math.sqrt(edges * devices)
    mixed = pl.pallas_call(
        functools.partial(mix_kernel, factor),
        out_shape=jax.ShapeDtypeStruct((devices, 96, LANES), jnp.bfloat16),
        in_specs=[smem] * 5 + [vmem],
        out_specs=vmem,
        scratch_shapes=[pltpu.SMEM((8, experts), jnp.float32)],
        compiler_params=params,
        name="mixing",
    )(own, *mixings, first)
    second = lax.all_to_all(mixed, axes, split_axis=0, concat_axis=0, tiled=True)

    messages, back, grad_experts = pl.pallas_call(
        message_kernel,
        out_shape=(
            jax.ShapeDtypeStruct((edges, channels), jnp.bfloat16),
            jax.ShapeDtypeStruct((edges, channels), jnp.bfloat16),
            jax.ShapeDtypeStruct((channels, width), jnp.float32),
        ),
        in_specs=[smem, smem, hbm, hbm, vmem],
        out_specs=(hbm, hbm, vmem),
        scratch_shapes=[
            held,
            held,
            held,
            held,
            pltpu.VMEM((2, channels, channels), jnp.bfloat16),
            pltpu.SMEM((slots,), jnp.int32),
            pltpu.SMEM((slots,), jnp.int32),
            pltpu.SemaphoreType.DMA((2, slots)),
            pltpu.SemaphoreType.DMA((2, slots)),
        ],
        compiler_params=params,
        cost_estimate=pl.CostEstimate(flops=4 * macs, bytes_accessed=24 * 2**20, transcendentals=0),
        name="messages",
    )(block_system, block_count, inputs, cotangent, second.reshape(64, 2, 96, LANES))
    return (messages, back, grad_experts.reshape(expert_weights.shape))


def solution(mesh):
    in_specs = (
        P(("dp", "expert"), None),
        P(("dp", "expert"), None),
        P("expert", None, None, None),
        P(),
        P("dp", None),
        P("dp"),
        P(("dp", "expert")),
        P(("dp", "expert")),
    )
    out_specs = (
        P(("dp", "expert"), None),
        P(("dp", "expert"), None),
        P("expert", None, None, None),
    )
    return jax.shard_map(local, mesh=mesh, in_specs=in_specs, out_specs=out_specs, check_vma=False)
```

```python
import functools
import math

import jax
import jax.numpy as jnp
from jax import lax
from jax.experimental import pallas as pl
from jax.experimental.pallas import tpu as pltpu
from jax.sharding import PartitionSpec as P

BLOCK = 128
LANES = 128
TILE_ROWS = 16
PAIR = 2 * BLOCK
STAGES = (1, 2, 3, 3)
VMEM_LIMIT = 32 * 1024 * 1024
FIRST = ((0,), (0,)), ((), ())
LAST = ((1,), (1,)), ((), ())


def f32_dot(a, b, dims=(((1,), (0,)), ((), ()))):
    return lax.dot_general(a, b, dims, preferred_element_type=jnp.float32)


def rows_of(index):
    return pl.ds(pl.multiple_of(index * BLOCK, BLOCK), BLOCK)


def place_blocks(system_ref, count_ref, slot_count, slot_block, start):
    blocks = system_ref.shape[0]

    def tally(b, total):
        return total + (system_ref[b] == 0).astype(jnp.int32)

    first = lax.fori_loop(0, blocks, tally, jnp.int32(0), unroll=True)
    pairs_first = (first + 1) // 2

    def clear(slot, _):
        slot_count[slot] = 0
        slot_block[slot] = 0
        return 0

    lax.fori_loop(0, slot_count.shape[0], clear, 0, unroll=True)
    for system in range(2):

        def give(b, slot):
            mine = system_ref[b] == system

            @pl.when(mine)
            def _():
                slot_count[slot] = count_ref[b]
                slot_block[slot] = b
                start(b, slot)

            return slot + mine.astype(jnp.int32)

        lax.fori_loop(0, blocks, give, jnp.int32(0) if system == 0 else pairs_first * 2)
    return pairs_first


def live_mask(slot_count, pair):
    row = lax.broadcasted_iota(jnp.int32, (BLOCK, 1), 0)
    parts = [(row < slot_count[2 * pair + i]).astype(jnp.float32) for i in range(2)]
    return jnp.concatenate(parts, axis=0).astype(jnp.bfloat16)


def grad_kernel(
    system_ref, count_ref, group_ref, x_hbm, g_hbm, w_hbm, out_hbm,
    x_held, g_held, out_ref, total, w_held, slot_count, slot_block, sems, w_sem, out_sems,
):
    width = x_hbm.shape[1] // 2
    slots = slot_count.shape[0]

    def copies(b, slot):
        for which, (source, held) in enumerate(((x_hbm, x_held), (g_hbm, g_held))):
            yield pltpu.make_async_copy(source.at[rows_of(b), :], held.at[rows_of(slot), :], sems.at[which, slot])

    def start(b, slot):
        for copy in copies(b, slot):
            copy.start()

    pairs_first = place_blocks(system_ref, count_ref, slot_count, slot_block, start)
    w_copy = pltpu.make_async_copy(w_hbm, w_held, w_sem)
    w_copy.start()
    total[...] = jnp.zeros_like(total)

    def clear(slot, _):
        @pl.when(slot_count[slot] == 0)
        def _():
            for held in (x_held, g_held):
                held[rows_of(slot), :] = jnp.zeros((BLOCK, 2 * width), held.dtype)

        return 0

    lax.fori_loop(0, slots, clear, 0)

    def arrive(slot, _):
        @pl.when(slot_count[slot] > 0)
        def _():
            for copy in copies(0, slot):
                copy.wait()

        return 0

    done = 0
    for stage in STAGES:
        lax.fori_loop(2 * done, 2 * (done + stage), arrive, 0)
        for pair in range(done, done + stage):
            rows = pl.ds(pair * PAIR, PAIR)
            system = (pair >= pairs_first).astype(jnp.int32)
            mask = live_mask(slot_count, pair)
            x_real = x_held[rows, :width] * mask
            x_imag = x_held[rows, width:] * mask
            g_real = g_held[rows, :width]
            g_imag = g_held[rows, width:]
            total[system, :, :width] += f32_dot(x_real + x_imag, g_real, FIRST)
            total[system, :, width:2 * width] += f32_dot(x_imag, g_imag - g_real, FIRST)
            total[system, :, 2 * width:] += f32_dot(x_real, g_real + g_imag, FIRST)
        done += stage

    w_copy.wait()
    own = group_ref[0]
    for half in range(2):
        pick = None
        for part in range(4):
            column = 256 * half + LANES * (part // 2)
            piece = w_held[:, column:column + LANES].astype(jnp.float32).reshape(64, TILE_ROWS, LANES)
            piece = piece[:, 8 * (part % 2):8 * (part % 2) + 8, :]
            pick = piece if pick is None else jnp.where(own == part, piece, pick)
        out_ref[64 * half:64 * half + 64, 64:72, :] = pick.astype(jnp.bfloat16)

    def copy_out(part):
        rows = (pl.ds(0, 32), pl.ds(32, 32), pl.ds(64, 8))[part]
        return pltpu.make_async_copy(out_ref.at[:, rows, :], out_hbm.at[:, rows, :], out_sems.at[part])

    copy_out(2).start()
    for system in range(2):
        for half in range(2):
            for block in range(2):
                column = 256 * half + LANES * block
                shared = total[system, :, column:column + LANES]
                real = total[system, :, width + column:width + column + LANES] + shared
                imag = total[system, :, 2 * width + column:2 * width + column + LANES] - shared
                row = system * 32 + block * TILE_ROWS
                for plane, piece in enumerate((real, imag)):
                    at = 64 * half + 32 * plane
                    out_ref[at:at + 32, row:row + TILE_ROWS, :] = piece.astype(jnp.bfloat16).reshape(
                        32, TILE_ROWS, LANES
                    )
        copy_out(system).start()
    for part in range(3):
        copy_out(part).wait()


def mix_kernel(factor, group_ref, mix0, mix1, mix2, mix3, in_ref, out_ref, mixing):
    own = group_ref[0]
    experts = mix0.shape[1]
    for j, part in enumerate((mix0, mix1, mix2, mix3)):
        at = (own ^ j) * 2

        def spread(e, _):
            mixing[at, e] = part[0, e]
            mixing[at + 1, e] = part[1, e]
            return 0

        lax.fori_loop(0, experts, spread, 0, unroll=True)

    def merge(e, totals):
        pieces = [in_ref[d * experts + e, 64:72, :].astype(jnp.float32) for d in range(4)]
        return tuple(totals[s * 4 + d] + mixing[s, e] * pieces[d] for s in range(8) for d in range(4))

    zero = jnp.zeros((8, LANES), jnp.float32)
    merged = lax.fori_loop(0, experts, merge, (zero,) * 32, unroll=2)
    packed = [
        jnp.concatenate([merged[(2 * d + s) * 4 + i] for s in range(2) for i in range(4)], axis=0).astype(jnp.bfloat16)
        for d in range(4)
    ]

    def gather(e, totals):
        for d in range(4):
            out_ref[d * experts + e, 0:64, :] = packed[d]
        return tuple(totals[d] + in_ref[d * experts + e, 0:64, :].astype(jnp.float32) for d in range(4))

    zero = jnp.zeros((64, LANES), jnp.float32)
    grads = lax.fori_loop(0, experts, gather, (zero,) * 4, unroll=2)
    grads = [grads[d] * factor for d in range(4)]

    def combine(e, _):
        result = zero[:32]
        for d in range(4):
            for s in range(2):
                result = result + mixing[2 * d + s, e] * grads[d][32 * s:32 * s + 32]
        result = result.astype(jnp.bfloat16)
        for d in range(4):
            out_ref[d * experts + e, 64:96, :] = result
        return 0

    lax.fori_loop(0, experts, combine, 0, unroll=2)


def message_kernel(
    system_ref, count_ref, x_ref, g_ref, in_ref, out_hbm, back_hbm, expert_hbm,
    out_held, back_held, expert_held, weight, slot_count, slot_block, sems, expert_sem,
):
    width = x_ref.shape[1] // 2
    slots = slot_count.shape[0]
    pairs_first = place_blocks(system_ref, count_ref, slot_count, slot_block, lambda b, slot: None)

    def columns(half, block, row):
        piece = in_ref[64 * half:64 * half + 64, row + block * TILE_ROWS:row + (block + 1) * TILE_ROWS, :]
        return piece.reshape(2 * width, LANES)

    for half in range(2):
        for block in range(2):
            column = 256 * half + LANES * block
            for system in range(2):
                piece = columns(half, block, 32 * system)
                real, imag = piece[:width], piece[width:]
                weight[system, 0, :, column:column + LANES] = real
                weight[system, 1, :, column:column + LANES] = imag - real
                weight[system, 2, :, column:column + LANES] = real + imag
            expert_held[:, column:column + LANES] = columns(half, block, 64).astype(jnp.float32)
    expert_copy = pltpu.make_async_copy(expert_held, expert_hbm, expert_sem)
    expert_copy.start()

    def copies(slot, b):
        for which, (held, target) in enumerate(((out_held, out_hbm), (back_held, back_hbm))):
            yield pltpu.make_async_copy(held.at[rows_of(slot), :], target.at[rows_of(b), :], sems.at[which, slot])

    for pair in range(slots // 2):
        rows = pl.ds(pair * PAIR, PAIR)
        system = (pair >= pairs_first).astype(jnp.int32)
        mask = live_mask(slot_count, pair)
        x_pair, g_pair = [
            jnp.concatenate([ref[rows_of(slot_block[2 * pair + i]), :] for i in range(2)], axis=0) * mask
            for ref in (x_ref, g_ref)
        ]
        x_real, x_imag = x_pair[:, :width], x_pair[:, width:]
        shared = f32_dot(x_real + x_imag, weight[system, 0])
        out_held[rows, :width] = (shared - f32_dot(x_imag, weight[system, 2])).astype(jnp.bfloat16)
        out_held[rows, width:] = (shared + f32_dot(x_real, weight[system, 1])).astype(jnp.bfloat16)
        g_real, g_imag = g_pair[:, :width], g_pair[:, width:]
        shared = f32_dot(g_real + g_imag, weight[system, 0], LAST)
        back_held[rows, :width] = (shared + f32_dot(g_imag, weight[system, 1], LAST)).astype(jnp.bfloat16)
        back_held[rows, width:] = (shared - f32_dot(g_real, weight[system, 2], LAST)).astype(jnp.bfloat16)
        for slot in (2 * pair, 2 * pair + 1):

            @pl.when(slot_count[slot] > 0)
            def _():
                for copy in copies(slot, slot_block[slot]):
                    copy.start()

    def finish(slot, _):
        @pl.when(slot_count[slot] > 0)
        def _():
            for copy in copies(slot, 0):
                copy.wait()

        return 0

    lax.fori_loop(0, slots, finish, 0)
    expert_copy.wait()


def local(
    inputs, cotangent, expert_weights, fidelity_table, system_weights, fidelity, block_system, block_count
):
    edges, channels = inputs.shape
    width = channels // 2
    blocks = block_system.shape[0]
    slots = blocks + 2
    axes = ("dp", "expert")
    devices = lax.axis_size("dp") * lax.axis_size("expert")
    experts = fidelity_table.shape[1]
    own = lax.axis_index("dp").astype(jnp.int32).reshape(1)

    picked = jnp.zeros(system_weights.shape, jnp.float32)
    for f in range(fidelity_table.shape[0]):
        picked = jnp.where((fidelity == f)[:, None], fidelity_table[f][None, :], picked)
    mixing = picked * system_weights
    mixings = [mixing] + [
        lax.ppermute(mixing, "dp", [(i, i ^ j) for i in range(4)]) for j in range(1, 4)
    ]

    smem = pl.BlockSpec(memory_space=pltpu.SMEM)
    vmem = pl.BlockSpec(memory_space=pltpu.VMEM)
    hbm = pl.BlockSpec(memory_space=pltpu.HBM)
    params = pltpu.CompilerParams(vmem_limit_bytes=VMEM_LIMIT)
    held = pltpu.VMEM((slots * BLOCK, channels), jnp.bfloat16)
    macs = edges * channels * channels
    tables = [pltpu.SMEM((slots,), jnp.int32), pltpu.SMEM((slots,), jnp.int32)]

    def exchange(chunks):
        got = lax.all_to_all(chunks, axes, split_axis=0, concat_axis=0, tiled=True)
        return pltpu.with_memory_space_constraint(got, pltpu.VMEM)

    pinned = [
        pltpu.with_memory_space_constraint(array, pltpu.HBM)
        for array in (inputs, cotangent, expert_weights.reshape(channels, width))
    ]
    partial = pl.pallas_call(
        grad_kernel,
        out_shape=pltpu.HBM((devices, 72, LANES), jnp.bfloat16),
        in_specs=[smem, smem, smem, hbm, hbm, hbm],
        out_specs=hbm,
        scratch_shapes=[
            held,
            held,
            pltpu.VMEM((devices, 72, LANES), jnp.bfloat16),
            pltpu.VMEM((2, width, 3 * width), jnp.float32),
            pltpu.VMEM((channels, width), jnp.bfloat16),
            *tables,
            pltpu.SemaphoreType.DMA((2, slots)),
            pltpu.SemaphoreType.DMA,
            pltpu.SemaphoreType.DMA((3,)),
        ],
        compiler_params=params,
        cost_estimate=pl.CostEstimate(flops=2 * macs, bytes_accessed=12 * 2**20, transcendentals=0),
        name="weight_gradients",
    )(*[pltpu.with_memory_space_constraint(table, pltpu.HBM) for table in (block_system, block_count)], own, *pinned)

    factor = experts / math.sqrt(edges * devices)
    mixed = pl.pallas_call(
        functools.partial(mix_kernel, factor),
        out_shape=pltpu.VMEM((devices, 96, LANES), jnp.bfloat16),
        in_specs=[smem] * 5 + [vmem],
        out_specs=vmem,
        scratch_shapes=[pltpu.SMEM((8, experts), jnp.float32)],
        compiler_params=params,
        name="mixing",
    )(own, *mixings, exchange(partial))

    messages, back, grad_experts = pl.pallas_call(
        message_kernel,
        out_shape=(
            jax.ShapeDtypeStruct((edges, channels), jnp.bfloat16),
            jax.ShapeDtypeStruct((edges, channels), jnp.bfloat16),
            jax.ShapeDtypeStruct((channels, width), jnp.float32),
        ),
        in_specs=[smem, smem, vmem, vmem, vmem],
        out_specs=(hbm, hbm, hbm),
        scratch_shapes=[
            held,
            held,
            pltpu.VMEM((channels, width), jnp.float32),
            pltpu.VMEM((2, 3, width, width), jnp.bfloat16),
            *tables,
            pltpu.SemaphoreType.DMA((2, slots)),
            pltpu.SemaphoreType.DMA,
        ],
        compiler_params=params,
        cost_estimate=pl.CostEstimate(flops=4 * macs, bytes_accessed=24 * 2**20, transcendentals=0),
        name="messages",
    )(block_system, block_count, pltpu.with_memory_space_constraint(inputs, pltpu.VMEM), pltpu.with_memory_space_constraint(cotangent, pltpu.VMEM), exchange(mixed))
    return (messages, back, grad_experts.reshape(expert_weights.shape))


def solution(mesh):
    in_specs = (
        P(("dp", "expert"), None),
        P(("dp", "expert"), None),
        P("expert", None, None, None),
        P(),
        P("dp", None),
        P("dp"),
        P(("dp", "expert")),
        P(("dp", "expert")),
    )
    out_specs = (
        P(("dp", "expert"), None),
        P(("dp", "expert"), None),
        P("expert", None, None, None),
    )
    return jax.shard_map(local, mesh=mesh, in_specs=in_specs, out_specs=out_specs, check_vma=False)
```

```python
import functools
import math

import jax
import jax.numpy as jnp
from jax import lax
from jax.experimental import pallas as pl
from jax.experimental.pallas import tpu as pltpu
from jax.sharding import PartitionSpec as P

BLOCK = 128
LANES = 128
TILE_ROWS = 16
PAIR = 2 * BLOCK
STAGES = (1, 2, 3, 3)
VMEM_LIMIT = 32 * 1024 * 1024
FIRST = ((0,), (0,)), ((), ())
LAST = ((1,), (1,)), ((), ())


def f32_dot(a, b, dims=(((1,), (0,)), ((), ()))):
    return lax.dot_general(a, b, dims, preferred_element_type=jnp.float32)


def rows_of(index):
    return pl.ds(pl.multiple_of(index * BLOCK, BLOCK), BLOCK)


def place_blocks(system_ref, count_ref, slot_count, slot_block):
    blocks = system_ref.shape[0]
    systems = [system_ref[b] for b in range(blocks)]
    pairs_first = (blocks - sum(systems) + 1) // 2
    for slot in range(slot_count.shape[0]):
        slot_count[slot] = 0
        slot_block[slot] = 0
    ends = [jnp.int32(0), pairs_first * 2]
    for b, system in enumerate(systems):
        slot = jnp.where(system == 0, ends[0], ends[1])
        slot_count[slot] = count_ref[b]
        slot_block[slot] = b
        ends = [ends[0] + 1 - system, ends[1] + system]
    return pairs_first


def live_mask(slot_count, pair):
    row = lax.broadcasted_iota(jnp.int32, (BLOCK, 1), 0)
    parts = [(row < slot_count[2 * pair + i]).astype(jnp.float32) for i in range(2)]
    return jnp.concatenate(parts, axis=0).astype(jnp.bfloat16)


def grad_kernel(
    system_ref, count_ref, group_ref, x_hbm, g_hbm, w_hbm, out_hbm,
    x_held, g_held, out_ref, total, w_held, slot_count, slot_block, sems, w_sem, out_sems,
):
    width = x_hbm.shape[1] // 2
    slots = slot_count.shape[0]

    def copies(b, slot):
        for which, (source, held) in enumerate(((x_hbm, x_held), (g_hbm, g_held))):
            yield pltpu.make_async_copy(source.at[rows_of(b), :], held.at[rows_of(slot), :], sems.at[which, slot])

    pairs_first = place_blocks(system_ref, count_ref, slot_count, slot_block)

    def start(slot, _):
        @pl.when(slot_count[slot] > 0)
        def _():
            for copy in copies(slot_block[slot], slot):
                copy.start()

        return 0

    lax.fori_loop(0, slots, start, 0)
    w_copy = pltpu.make_async_copy(w_hbm, w_held, w_sem)
    w_copy.start()
    total[...] = jnp.zeros_like(total)

    def clear(slot, _):
        @pl.when(slot_count[slot] == 0)
        def _():
            for held in (x_held, g_held):
                held[rows_of(slot), :] = jnp.zeros((BLOCK, 2 * width), held.dtype)

        return 0

    lax.fori_loop(0, slots, clear, 0)

    def arrive(slot, _):
        @pl.when(slot_count[slot] > 0)
        def _():
            for copy in copies(0, slot):
                copy.wait()

        return 0

    done = 0
    for stage in STAGES:
        lax.fori_loop(2 * done, 2 * (done + stage), arrive, 0)
        for pair in range(done, done + stage):
            rows = pl.ds(pair * PAIR, PAIR)
            system = (pair >= pairs_first).astype(jnp.int32)
            mask = live_mask(slot_count, pair)
            x_real = x_held[rows, :width] * mask
            x_imag = x_held[rows, width:] * mask
            g_real = g_held[rows, :width]
            g_imag = g_held[rows, width:]
            total[system, :, :width] += f32_dot(x_real + x_imag, g_real, FIRST)
            total[system, :, width:2 * width] += f32_dot(x_imag, g_imag - g_real, FIRST)
            total[system, :, 2 * width:] += f32_dot(x_real, g_real + g_imag, FIRST)
        done += stage

    w_copy.wait()
    own = group_ref[0]
    for half in range(2):
        pick = None
        for part in range(4):
            column = 256 * half + LANES * (part // 2)
            piece = w_held[:, column:column + LANES].astype(jnp.float32).reshape(64, TILE_ROWS, LANES)
            piece = piece[:, 8 * (part % 2):8 * (part % 2) + 8, :]
            pick = piece if pick is None else jnp.where(own == part, piece, pick)
        out_ref[64 * half:64 * half + 64, 64:72, :] = pick.astype(jnp.bfloat16)

    def copy_out(part):
        rows = (pl.ds(0, 32), pl.ds(32, 32), pl.ds(64, 8))[part]
        return pltpu.make_async_copy(out_ref.at[:, rows, :], out_hbm.at[:, rows, :], out_sems.at[part])

    copy_out(2).start()
    for system in range(2):
        for half in range(2):
            for block in range(2):
                column = 256 * half + LANES * block
                shared = total[system, :, column:column + LANES]
                real = total[system, :, width + column:width + column + LANES] + shared
                imag = total[system, :, 2 * width + column:2 * width + column + LANES] - shared
                row = system * 32 + block * TILE_ROWS
                for plane, piece in enumerate((real, imag)):
                    at = 64 * half + 32 * plane
                    out_ref[at:at + 32, row:row + TILE_ROWS, :] = piece.astype(jnp.bfloat16).reshape(
                        32, TILE_ROWS, LANES
                    )
        copy_out(system).start()
    for part in range(3):
        copy_out(part).wait()


def mix_kernel(factor, group_ref, mix0, mix1, mix2, mix3, in_ref, out_ref, mixing):
    own = group_ref[0]
    experts = mix0.shape[1]
    for j, part in enumerate((mix0, mix1, mix2, mix3)):
        at = (own ^ j) * 2

        def spread(e, _):
            mixing[at, e] = part[0, e]
            mixing[at + 1, e] = part[1, e]
            return 0

        lax.fori_loop(0, experts, spread, 0, unroll=True)

    def merge(e, totals):
        pieces = [in_ref[d * experts + e, 64:72, :].astype(jnp.float32) for d in range(4)]
        return tuple(totals[s * 4 + d] + mixing[s, e] * pieces[d] for s in range(8) for d in range(4))

    zero = jnp.zeros((8, LANES), jnp.float32)
    merged = lax.fori_loop(0, experts, merge, (zero,) * 32, unroll=2)
    packed = [
        jnp.concatenate([merged[(2 * d + s) * 4 + i] for s in range(2) for i in range(4)], axis=0).astype(jnp.bfloat16)
        for d in range(4)
    ]

    def gather(e, totals):
        for d in range(4):
            out_ref[d * experts + e, 0:64, :] = packed[d]
        return tuple(totals[d] + in_ref[d * experts + e, 0:64, :].astype(jnp.float32) for d in range(4))

    zero = jnp.zeros((64, LANES), jnp.float32)
    grads = lax.fori_loop(0, experts, gather, (zero,) * 4, unroll=2)
    grads = [grads[d] * factor for d in range(4)]

    def combine(e, _):
        result = zero[:32]
        for d in range(4):
            for s in range(2):
                result = result + mixing[2 * d + s, e] * grads[d][32 * s:32 * s + 32]
        for d in range(4):
            out_ref[d * experts + e, 64:72, :] = result[8 * d:8 * d + 8].astype(jnp.bfloat16)
        return 0

    lax.fori_loop(0, experts, combine, 0, unroll=2)


def message_kernel(
    system_ref, count_ref, x_ref, g_ref, in_ref, out_hbm, back_hbm,
    out_held, back_held, weight, slot_count, slot_block, sems,
):
    width = x_ref.shape[1] // 2
    slots = slot_count.shape[0]
    pairs_first = place_blocks(system_ref, count_ref, slot_count, slot_block)

    for half in range(2):
        for block in range(2):
            column = 256 * half + LANES * block
            for system in range(2):
                row = 32 * system + block * TILE_ROWS
                piece = in_ref[64 * half:64 * half + 64, row:row + TILE_ROWS, :].reshape(2 * width, LANES)
                real, imag = piece[:width], piece[width:]
                weight[system, 0, :, column:column + LANES] = real
                weight[system, 1, :, column:column + LANES] = imag - real
                weight[system, 2, :, column:column + LANES] = real + imag

    def copies(slot, b):
        for which, (held, target) in enumerate(((out_held, out_hbm), (back_held, back_hbm))):
            yield pltpu.make_async_copy(held.at[rows_of(slot), :], target.at[rows_of(b), :], sems.at[which, slot])

    for pair in range(slots // 2):
        rows = pl.ds(pair * PAIR, PAIR)
        system = (pair >= pairs_first).astype(jnp.int32)
        mask = live_mask(slot_count, pair)
        x_pair, g_pair = [
            jnp.concatenate([ref[rows_of(slot_block[2 * pair + i]), :] for i in range(2)], axis=0) * mask
            for ref in (x_ref, g_ref)
        ]
        x_real, x_imag = x_pair[:, :width], x_pair[:, width:]
        shared = f32_dot(x_real + x_imag, weight[system, 0])
        out_held[rows, :width] = (shared - f32_dot(x_imag, weight[system, 2])).astype(jnp.bfloat16)
        out_held[rows, width:] = (shared + f32_dot(x_real, weight[system, 1])).astype(jnp.bfloat16)
        g_real, g_imag = g_pair[:, :width], g_pair[:, width:]
        shared = f32_dot(g_real + g_imag, weight[system, 0], LAST)
        back_held[rows, :width] = (shared + f32_dot(g_imag, weight[system, 1], LAST)).astype(jnp.bfloat16)
        back_held[rows, width:] = (shared - f32_dot(g_real, weight[system, 2], LAST)).astype(jnp.bfloat16)
        for slot in (2 * pair, 2 * pair + 1):

            @pl.when(slot_count[slot] > 0)
            def _():
                for copy in copies(slot, slot_block[slot]):
                    copy.start()

    def finish(slot, _):
        @pl.when(slot_count[slot] > 0)
        def _():
            for copy in copies(slot, 0):
                copy.wait()

        return 0

    lax.fori_loop(0, slots, finish, 0)


def expert_kernel(group_ref, part0, part1, part2, part3, out_hbm, held, sems):
    own = group_ref[0]

    def copy_out(half):
        columns = pl.ds(256 * half, 256)
        return pltpu.make_async_copy(held.at[:, columns], out_hbm.at[:, columns], sems.at[half])

    for half in range(2):
        parts = [p[64 * half:64 * half + 64, :, :].astype(jnp.float32) for p in (part0, part1, part2, part3)]
        for block in range(2):
            quarters = []
            for d in (2 * block, 2 * block + 1):
                far = own ^ d
                quarters.append(
                    jnp.where(far < 2, jnp.where(far == 0, parts[0], parts[1]), jnp.where(far == 2, parts[2], parts[3]))
                )
            column = 256 * half + LANES * block
            held[:, column:column + LANES] = jnp.concatenate(quarters, axis=1).reshape(held.shape[0], LANES)
        copy_out(half).start()
    for half in range(2):
        copy_out(half).wait()


def local(
    inputs, cotangent, expert_weights, fidelity_table, system_weights, fidelity, block_system, block_count
):
    edges, channels = inputs.shape
    width = channels // 2
    blocks = block_system.shape[0]
    slots = blocks + 2
    axes = ("dp", "expert")
    devices = lax.axis_size("dp") * lax.axis_size("expert")
    experts = fidelity_table.shape[1]
    own = lax.axis_index("dp").astype(jnp.int32).reshape(1)

    picked = jnp.zeros(system_weights.shape, jnp.float32)
    for f in range(fidelity_table.shape[0]):
        picked = jnp.where((fidelity == f)[:, None], fidelity_table[f][None, :], picked)
    mixing = picked * system_weights
    mixings = [mixing] + [
        lax.ppermute(mixing, "dp", [(i, i ^ j) for i in range(4)]) for j in range(1, 4)
    ]

    smem = pl.BlockSpec(memory_space=pltpu.SMEM)
    vmem = pl.BlockSpec(memory_space=pltpu.VMEM)
    hbm = pl.BlockSpec(memory_space=pltpu.HBM)
    params = pltpu.CompilerParams(vmem_limit_bytes=VMEM_LIMIT)
    held = pltpu.VMEM((slots * BLOCK, channels), jnp.bfloat16)
    macs = edges * channels * channels
    tables = [pltpu.SMEM((slots,), jnp.int32), pltpu.SMEM((slots,), jnp.int32)]

    def exchange(chunks):
        return lax.all_to_all(chunks, axes, split_axis=0, concat_axis=0, tiled=True)

    pinned = [
        pltpu.with_memory_space_constraint(array, pltpu.HBM)
        for array in (inputs, cotangent, expert_weights.reshape(channels, width))
    ]
    partial = pl.pallas_call(
        grad_kernel,
        out_shape=pltpu.HBM((devices, 72, LANES), jnp.bfloat16),
        in_specs=[smem, smem, smem, hbm, hbm, hbm],
        out_specs=hbm,
        scratch_shapes=[
            held,
            held,
            pltpu.VMEM((devices, 72, LANES), jnp.bfloat16),
            pltpu.VMEM((2, width, 3 * width), jnp.float32),
            pltpu.VMEM((channels, width), jnp.bfloat16),
            *tables,
            pltpu.SemaphoreType.DMA((2, slots)),
            pltpu.SemaphoreType.DMA,
            pltpu.SemaphoreType.DMA((3,)),
        ],
        compiler_params=params,
        cost_estimate=pl.CostEstimate(flops=2 * macs, bytes_accessed=12 * 2**20, transcendentals=0),
        name="weight_gradients",
    )(*[pltpu.with_memory_space_constraint(table, pltpu.HBM) for table in (block_system, block_count)], own, *pinned)

    factor = experts / math.sqrt(edges * devices)
    arrived = exchange(partial)
    mixed = pl.pallas_call(
        functools.partial(mix_kernel, factor),
        out_shape=pltpu.VMEM((devices, 72, LANES), jnp.bfloat16),
        in_specs=[smem] * 5 + [vmem],
        out_specs=vmem,
        scratch_shapes=[pltpu.SMEM((8, experts), jnp.float32)],
        compiler_params=params,
        name="mixing",
    )(own, *mixings, pltpu.with_memory_space_constraint(arrived, pltpu.VMEM))

    received = exchange(mixed)
    quarter = received[:, 64:72, :]
    quarters = [quarter] + [
        lax.ppermute(quarter, "dp", [(i, i ^ j) for i in range(4)]) for j in range(1, 4)
    ]
    messages, back = pl.pallas_call(
        message_kernel,
        out_shape=(
            jax.ShapeDtypeStruct((edges, channels), jnp.bfloat16),
            jax.ShapeDtypeStruct((edges, channels), jnp.bfloat16),
        ),
        in_specs=[smem, smem, vmem, vmem, vmem],
        out_specs=(hbm, hbm),
        scratch_shapes=[
            held,
            held,
            pltpu.VMEM((2, 3, width, width), jnp.bfloat16),
            *tables,
            pltpu.SemaphoreType.DMA((2, slots)),
        ],
        compiler_params=params,
        cost_estimate=pl.CostEstimate(flops=4 * macs, bytes_accessed=24 * 2**20, transcendentals=0),
        name="messages",
    )(block_system, block_count, pltpu.with_memory_space_constraint(inputs, pltpu.VMEM), pltpu.with_memory_space_constraint(cotangent, pltpu.VMEM), pltpu.with_memory_space_constraint(received, pltpu.VMEM))
    grad_experts = pl.pallas_call(
        expert_kernel,
        out_shape=jax.ShapeDtypeStruct((channels, width), jnp.float32),
        in_specs=[smem, vmem, vmem, vmem, vmem],
        out_specs=hbm,
        scratch_shapes=[pltpu.VMEM((channels, width), jnp.float32), pltpu.SemaphoreType.DMA((2,))],
        compiler_params=params,
        name="expert_gradients",
    )(own, *[pltpu.with_memory_space_constraint(part, pltpu.VMEM) for part in quarters])
    return (messages, back, grad_experts.reshape(expert_weights.shape))


def solution(mesh):
    in_specs = (
        P(("dp", "expert"), None),
        P(("dp", "expert"), None),
        P("expert", None, None, None),
        P(),
        P("dp", None),
        P("dp"),
        P(("dp", "expert")),
        P(("dp", "expert")),
    )
    out_specs = (
        P(("dp", "expert"), None),
        P(("dp", "expert"), None),
        P("expert", None, None, None),
    )
    return jax.shard_map(local, mesh=mesh, in_specs=in_specs, out_specs=out_specs, check_vma=False)
```

```python
import functools
import math

import jax
import jax.numpy as jnp
from jax import lax
from jax.experimental import pallas as pl
from jax.experimental.pallas import tpu as pltpu
from jax.sharding import PartitionSpec as P

BLOCK = 128
LANES = 128
TILE_ROWS = 16
PAIR = 2 * BLOCK
STAGES = (1, 2, 3, 3)
UNROLL = 4
VMEM_LIMIT = 32 * 1024 * 1024
FIRST = ((0,), (0,)), ((), ())
LAST = ((1,), (1,)), ((), ())


def f32_dot(a, b, dims=(((1,), (0,)), ((), ()))):
    return lax.dot_general(a, b, dims, preferred_element_type=jnp.float32)


def rows_of(index):
    return pl.ds(pl.multiple_of(index * BLOCK, BLOCK), BLOCK)


def pair_up(system_ref, count_ref, pair_system, slot_block, slot_count):
    blocks = system_ref.shape[0]
    pair = jnp.int32(0)
    waiting = [jnp.int32(-1), jnp.int32(-1)]
    for b in range(blocks):
        system = system_ref[b]
        mate = jnp.where(system == 0, waiting[0], waiting[1])
        paired = mate >= 0
        near = jnp.maximum(mate, 0)
        pair_system[pair] = system
        slot_block[2 * pair] = near
        slot_block[2 * pair + 1] = b
        slot_count[2 * pair] = count_ref[near]
        slot_count[2 * pair + 1] = count_ref[b]
        pair += paired.astype(jnp.int32)
        left = jnp.where(paired, -1, b)
        waiting = [jnp.where(system == s, left, waiting[s]) for s in range(2)]
    for system in range(2):
        alone = waiting[system] >= 0
        near = jnp.maximum(waiting[system], 0)
        pair_system[pair] = system
        slot_block[2 * pair] = near
        slot_block[2 * pair + 1] = near
        slot_count[2 * pair] = jnp.where(alone, count_ref[near], 0)
        slot_count[2 * pair + 1] = 0
        pair += alone.astype(jnp.int32)


def table_copies(system_hbm, count_hbm, system_ref, count_ref, sems):
    return [
        pltpu.make_async_copy(system_hbm, system_ref, sems.at[0]),
        pltpu.make_async_copy(count_hbm, count_ref, sems.at[1]),
    ]


def masked_pair(refs, slot_block, slot_count, pair):
    row = lax.broadcasted_iota(jnp.int32, (BLOCK, 1), 0)
    live = [(row < slot_count[2 * pair + i]).astype(jnp.float32) for i in range(2)]
    mask = jnp.concatenate(live, axis=0).astype(jnp.bfloat16)
    return mask, *[
        jnp.concatenate([ref[rows_of(slot_block[2 * pair + i]), :] for i in range(2)], axis=0) for ref in refs
    ]


def grad_kernel(
    system_hbm, count_hbm, x_hbm, g_hbm, w_hbm, out_hbm,
    x_held, g_held, out_ref, total, w_held, system_ref, count_ref, pair_system, slot_block, slot_count,
    table_sems, sems, w_sem, out_sems,
):
    width = x_hbm.shape[1] // 2
    chunks = x_hbm.shape[0] // PAIR
    tables = table_copies(system_hbm, count_hbm, system_ref, count_ref, table_sems)
    for copy in tables:
        copy.start()

    def copies(chunk):
        rows = pl.ds(chunk * PAIR, PAIR)
        for which, (source, held) in enumerate(((x_hbm, x_held), (g_hbm, g_held))):
            yield pltpu.make_async_copy(source.at[rows, :], held.at[rows, :], sems.at[which, chunk])

    w_copy = pltpu.make_async_copy(w_hbm, w_held, w_sem)
    for chunk in range(chunks):
        for copy in copies(chunk):
            copy.start()
        if chunk == chunks // 2:
            w_copy.start()
    total[...] = jnp.zeros_like(total)
    for copy in tables:
        copy.wait()
    pair_up(system_ref, count_ref, pair_system, slot_block, slot_count)

    def copy_out(rows, lines, sem):
        return pltpu.make_async_copy(out_ref.at[rows, lines, :], out_hbm.at[rows, lines, :], out_sems.at[sem])

    sent = [copy_out(pl.ds(0, 128), pl.ds(64, 8), 0)]

    def pack_weights():
        w_copy.wait()
        own = lax.axis_index("dp")
        for half in range(2):
            pick = None
            for part in range(4):
                column = 256 * half + LANES * (part // 2)
                piece = w_held[:, column:column + LANES].astype(jnp.float32).reshape(64, TILE_ROWS, LANES)
                piece = piece[:, 8 * (part % 2):8 * (part % 2) + 8, :]
                pick = piece if pick is None else jnp.where(own == part, piece, pick)
            out_ref[64 * half:64 * half + 64, 64:72, :] = pick.astype(jnp.bfloat16)
        sent[0].start()

    done = arrived = 0
    for stage in STAGES:
        needed = min(done + stage + 1, chunks)
        for chunk in range(arrived, needed):
            for copy in copies(chunk):
                copy.wait()
        arrived = needed
        for pair in range(done, done + stage):
            mask, x_pair, g_pair = masked_pair((x_held, g_held), slot_block, slot_count, pair)
            system = pair_system[pair]
            x_real, x_imag = x_pair[:, :width] * mask, x_pair[:, width:] * mask
            g_real, g_imag = g_pair[:, :width], g_pair[:, width:]
            total[system, :, :width] += f32_dot(x_real + x_imag, g_real, FIRST)
            total[system, :, width:2 * width] += f32_dot(x_imag, g_imag - g_real, FIRST)
            total[system, :, 2 * width:] += f32_dot(x_real, g_real + g_imag, FIRST)
        done += stage
        if done == sum(STAGES[:-1]):
            pack_weights()

    for system in range(2):
        for half in range(2):
            for block in range(2):
                column = 256 * half + LANES * block
                shared = total[system, :, column:column + LANES]
                real = total[system, :, width + column:width + column + LANES] + shared
                imag = total[system, :, 2 * width + column:2 * width + column + LANES] - shared
                row = system * 32 + block * TILE_ROWS
                for plane, piece in enumerate((real, imag)):
                    at = 64 * half + 32 * plane
                    out_ref[at:at + 32, row:row + TILE_ROWS, :] = piece.astype(jnp.bfloat16).reshape(
                        32, TILE_ROWS, LANES
                    )
            sent.append(copy_out(pl.ds(64 * half, 64), pl.ds(32 * system, 32), len(sent)))
            sent[-1].start()
    for copy in sent:
        copy.wait()


def mix_kernel(factor, mix0, mix1, mix2, mix3, in_ref, out_ref):
    parts = (mix0, mix1, mix2, mix3)
    experts = mix0.shape[1]
    own = lax.axis_index("dp")
    at = [(own ^ j) * experts for j in range(4)]

    def merge(e, totals):
        pieces = [in_ref[d * experts + e, 64:72, :].astype(jnp.float32) for d in range(4)]
        return tuple(
            totals[s * 4 + d] + parts[s // 2][s % 2, e] * pieces[d] for s in range(8) for d in range(4)
        )

    zero = jnp.zeros((8, LANES), jnp.float32)
    merged = lax.fori_loop(0, experts, merge, (zero,) * 32, unroll=UNROLL)
    packed = [
        jnp.concatenate([merged[(2 * j + s) * 4 + i] for s in range(2) for i in range(4)], axis=0).astype(jnp.bfloat16)
        for j in range(4)
    ]

    def gather(e, totals):
        for j in range(4):
            out_ref[at[j] + e, 0:64, :] = packed[j]
        return tuple(totals[j] + in_ref[at[j] + e, 0:64, :].astype(jnp.float32) for j in range(4))

    zero = jnp.zeros((64, LANES), jnp.float32)
    grads = lax.fori_loop(0, experts, gather, (zero,) * 4, unroll=UNROLL)
    grads = [grad * factor for grad in grads]

    def combine(e, _):
        terms = [parts[j][s, e] * grads[j][32 * s:32 * s + 32] for j in range(4) for s in range(2)]
        result = sum(terms[1:], terms[0])
        for d in range(4):
            out_ref[d * experts + e, 64:72, :] = result[8 * d:8 * d + 8].astype(jnp.bfloat16)
        return 0

    lax.fori_loop(0, experts, combine, 0, unroll=UNROLL)


def message_kernel(
    system_hbm, count_hbm, x_ref, g_ref, in_ref, out_hbm, back_hbm,
    out_held, back_held, weight, system_ref, count_ref, pair_system, slot_block, slot_count, table_sems, sems,
):
    width = x_ref.shape[1] // 2
    pairs = out_held.shape[0] // PAIR
    tables = table_copies(system_hbm, count_hbm, system_ref, count_ref, table_sems)
    for copy in tables:
        copy.start()

    for half in range(2):
        for block in range(2):
            column = 256 * half + LANES * block
            for system in range(2):
                row = 32 * system + block * TILE_ROWS
                piece = in_ref[64 * half:64 * half + 64, row:row + TILE_ROWS, :].reshape(2 * width, LANES)
                real, imag = piece[:width], piece[width:]
                weight[system, 0, :, column:column + LANES] = real
                weight[system, 1, :, column:column + LANES] = imag - real
                weight[system, 2, :, column:column + LANES] = real + imag

    for copy in tables:
        copy.wait()
    pair_up(system_ref, count_ref, pair_system, slot_block, slot_count)

    def copies(slot, b):
        for which, (held, target) in enumerate(((out_held, out_hbm), (back_held, back_hbm))):
            yield pltpu.make_async_copy(held.at[rows_of(slot), :], target.at[rows_of(b), :], sems.at[which, slot])

    for pair in range(pairs):
        rows = pl.ds(pair * PAIR, PAIR)
        system = pair_system[pair]
        mask, x_pair, g_pair = masked_pair((x_ref, g_ref), slot_block, slot_count, pair)
        x_real, x_imag = x_pair[:, :width] * mask, x_pair[:, width:] * mask
        shared = f32_dot(x_real + x_imag, weight[system, 0])
        out_held[rows, :width] = (shared - f32_dot(x_imag, weight[system, 2])).astype(jnp.bfloat16)
        out_held[rows, width:] = (shared + f32_dot(x_real, weight[system, 1])).astype(jnp.bfloat16)
        g_real, g_imag = g_pair[:, :width] * mask, g_pair[:, width:] * mask
        shared = f32_dot(g_real + g_imag, weight[system, 0], LAST)
        back_held[rows, :width] = (shared + f32_dot(g_imag, weight[system, 1], LAST)).astype(jnp.bfloat16)
        back_held[rows, width:] = (shared - f32_dot(g_real, weight[system, 2], LAST)).astype(jnp.bfloat16)
        for slot in (2 * pair, 2 * pair + 1):

            @pl.when(slot_count[slot] > 0)
            def _():
                for copy in copies(slot, slot_block[slot]):
                    copy.start()

    def finish(slot, _):
        @pl.when(slot_count[slot] > 0)
        def _():
            for copy in copies(slot, 0):
                copy.wait()

        return 0

    lax.fori_loop(0, 2 * pairs, finish, 0)


def expert_kernel(part0, part1, part2, part3, out_hbm, held, sems):
    own = lax.axis_index("dp")

    def copy_out(half):
        columns = pl.ds(256 * half, 256)
        return pltpu.make_async_copy(held.at[:, columns], out_hbm.at[:, columns], sems.at[half])

    for half in range(2):
        parts = [p[64 * half:64 * half + 64, :, :].astype(jnp.float32) for p in (part0, part1, part2, part3)]
        for block in range(2):
            quarters = []
            for d in (2 * block, 2 * block + 1):
                far = own ^ d
                quarters.append(
                    jnp.where(far < 2, jnp.where(far == 0, parts[0], parts[1]), jnp.where(far == 2, parts[2], parts[3]))
                )
            column = 256 * half + LANES * block
            held[:, column:column + LANES] = jnp.concatenate(quarters, axis=1).reshape(held.shape[0], LANES)
        copy_out(half).start()
    for half in range(2):
        copy_out(half).wait()


def local(
    inputs, cotangent, expert_weights, fidelity_table, system_weights, fidelity, block_system, block_count
):
    edges, channels = inputs.shape
    width = channels // 2
    blocks = block_system.shape[0]
    pairs = blocks // 2 + 1
    axes = ("dp", "expert")
    devices = lax.axis_size("dp") * lax.axis_size("expert")
    experts = fidelity_table.shape[1]

    picked = jnp.zeros(system_weights.shape, jnp.float32)
    for f in range(fidelity_table.shape[0]):
        picked = jnp.where((fidelity == f)[:, None], fidelity_table[f][None, :], picked)
    mixing = picked * system_weights
    mixings = [mixing] + [
        lax.ppermute(mixing, "dp", [(i, i ^ j) for i in range(4)]) for j in range(1, 4)
    ]

    smem = pl.BlockSpec(memory_space=pltpu.SMEM)
    vmem = pl.BlockSpec(memory_space=pltpu.VMEM)
    hbm = pl.BlockSpec(memory_space=pltpu.HBM)
    params = pltpu.CompilerParams(vmem_limit_bytes=VMEM_LIMIT)
    held = pltpu.VMEM((pairs * PAIR, channels), jnp.bfloat16)
    whole = pltpu.VMEM((edges, channels), jnp.bfloat16)
    macs = edges * channels * channels
    tables = [pltpu.SMEM((size,), jnp.int32) for size in (blocks, blocks, pairs + 1, 2 * pairs + 2, 2 * pairs + 2)]

    def exchange(chunks):
        return lax.all_to_all(chunks, axes, split_axis=0, concat_axis=0, tiled=True)

    pinned = [
        pltpu.with_memory_space_constraint(array, pltpu.HBM)
        for array in (block_system, block_count, inputs, cotangent, expert_weights.reshape(channels, width))
    ]
    partial = pl.pallas_call(
        grad_kernel,
        out_shape=pltpu.HBM((devices, 72, LANES), jnp.bfloat16),
        in_specs=[hbm] * 5,
        out_specs=hbm,
        scratch_shapes=[
            whole,
            whole,
            pltpu.VMEM((devices, 72, LANES), jnp.bfloat16),
            pltpu.VMEM((2, width, 3 * width), jnp.float32),
            pltpu.VMEM((channels, width), jnp.bfloat16),
            *tables,
            pltpu.SemaphoreType.DMA((2,)),
            pltpu.SemaphoreType.DMA((2, edges // PAIR)),
            pltpu.SemaphoreType.DMA,
            pltpu.SemaphoreType.DMA((5,)),
        ],
        compiler_params=params,
        cost_estimate=pl.CostEstimate(flops=2 * macs, bytes_accessed=12 * 2**20, transcendentals=0),
        name="weight_gradients",
    )(*pinned)

    factor = experts / math.sqrt(edges * devices)
    arrived = exchange(partial)
    mixed = pl.pallas_call(
        functools.partial(mix_kernel, factor),
        out_shape=pltpu.VMEM((devices, 72, LANES), jnp.bfloat16),
        in_specs=[smem] * 4 + [vmem],
        out_specs=vmem,
        compiler_params=params,
        name="mixing",
    )(*mixings, pltpu.with_memory_space_constraint(arrived, pltpu.VMEM))

    received = exchange(mixed)
    quarter = received[:, 64:72, :]
    quarters = [quarter] + [
        lax.ppermute(quarter, "dp", [(i, i ^ j) for i in range(4)]) for j in range(1, 4)
    ]
    messages, back = pl.pallas_call(
        message_kernel,
        out_shape=(
            jax.ShapeDtypeStruct((edges, channels), jnp.bfloat16),
            jax.ShapeDtypeStruct((edges, channels), jnp.bfloat16),
        ),
        in_specs=[hbm, hbm, vmem, vmem, vmem],
        out_specs=(hbm, hbm),
        scratch_shapes=[
            held,
            held,
            pltpu.VMEM((2, 3, width, width), jnp.bfloat16),
            *tables,
            pltpu.SemaphoreType.DMA((2,)),
            pltpu.SemaphoreType.DMA((2, 2 * pairs)),
        ],
        compiler_params=params,
        cost_estimate=pl.CostEstimate(flops=4 * macs, bytes_accessed=24 * 2**20, transcendentals=0),
        name="messages",
    )(*pinned[:2], pltpu.with_memory_space_constraint(inputs, pltpu.VMEM), pltpu.with_memory_space_constraint(cotangent, pltpu.VMEM), pltpu.with_memory_space_constraint(received, pltpu.VMEM))
    grad_experts = pl.pallas_call(
        expert_kernel,
        out_shape=jax.ShapeDtypeStruct((channels, width), jnp.float32),
        in_specs=[vmem] * 4,
        out_specs=hbm,
        scratch_shapes=[pltpu.VMEM((channels, width), jnp.float32), pltpu.SemaphoreType.DMA((2,))],
        compiler_params=params,
        name="expert_gradients",
    )(*[pltpu.with_memory_space_constraint(part, pltpu.VMEM) for part in quarters])
    return (messages, back, grad_experts.reshape(expert_weights.shape))


def solution(mesh):
    in_specs = (
        P(("dp", "expert"), None),
        P(("dp", "expert"), None),
        P("expert", None, None, None),
        P(),
        P("dp", None),
        P("dp"),
        P(("dp", "expert")),
        P(("dp", "expert")),
    )
    out_specs = (
        P(("dp", "expert"), None),
        P(("dp", "expert"), None),
        P("expert", None, None, None),
    )
    return jax.shard_map(local, mesh=mesh, in_specs=in_specs, out_specs=out_specs, check_vma=False)
```

```python
import functools
import math

import jax
import jax.numpy as jnp
from jax import lax
from jax.experimental import pallas as pl
from jax.experimental.pallas import tpu as pltpu
from jax.sharding import PartitionSpec as P

BLOCK = 128
LANES = 128
TILE_ROWS = 16
PAIR = 2 * BLOCK
STAGES = (1, 2, 3, 3)
UNROLL = 4
VMEM_LIMIT = 32 * 1024 * 1024
FIRST = ((0,), (0,)), ((), ())
LAST = ((1,), (1,)), ((), ())


def f32_dot(a, b, dims=(((1,), (0,)), ((), ()))):
    return lax.dot_general(a, b, dims, preferred_element_type=jnp.float32)


def rows_of(index):
    return pl.ds(pl.multiple_of(index * BLOCK, BLOCK), BLOCK)


def pair_up(system_ref, count_ref, pair_system, slot_block, slot_count):
    blocks = system_ref.shape[0]
    pair = jnp.int32(0)
    waiting = [jnp.int32(-1), jnp.int32(-1)]
    for b in range(blocks):
        system = system_ref[b]
        mate = jnp.where(system == 0, waiting[0], waiting[1])
        paired = mate >= 0
        near = jnp.maximum(mate, 0)
        pair_system[pair] = system
        slot_block[2 * pair] = near
        slot_block[2 * pair + 1] = b
        slot_count[2 * pair] = count_ref[near]
        slot_count[2 * pair + 1] = count_ref[b]
        pair += paired.astype(jnp.int32)
        left = jnp.where(paired, -1, b)
        waiting = [jnp.where(system == s, left, waiting[s]) for s in range(2)]
    for system in range(2):
        alone = waiting[system] >= 0
        near = jnp.maximum(waiting[system], 0)
        pair_system[pair] = system
        slot_block[2 * pair] = near
        slot_block[2 * pair + 1] = near
        slot_count[2 * pair] = jnp.where(alone, count_ref[near], 0)
        slot_count[2 * pair + 1] = 0
        pair += alone.astype(jnp.int32)


def table_copies(system_hbm, count_hbm, system_ref, count_ref, sems):
    return [
        pltpu.make_async_copy(system_hbm, system_ref, sems.at[0]),
        pltpu.make_async_copy(count_hbm, count_ref, sems.at[1]),
    ]


def masked_pair(refs, slot_block, slot_count, pair):
    row = lax.broadcasted_iota(jnp.int32, (BLOCK, 1), 0)
    live = [(row < slot_count[2 * pair + i]).astype(jnp.float32) for i in range(2)]
    mask = jnp.concatenate(live, axis=0).astype(jnp.bfloat16)
    return mask, *[
        jnp.concatenate([ref[rows_of(slot_block[2 * pair + i]), :] for i in range(2)], axis=0) for ref in refs
    ]


def grad_kernel(
    system_hbm, count_hbm, x_hbm, g_hbm, w_hbm, out_hbm,
    x_held, g_held, out_ref, total, w_held, system_ref, count_ref, pair_system, slot_block, slot_count,
    table_sems, sems, w_sem, out_sems,
):
    width = x_hbm.shape[1] // 2
    chunks = x_hbm.shape[0] // PAIR
    tables = table_copies(system_hbm, count_hbm, system_ref, count_ref, table_sems)
    for copy in tables:
        copy.start()

    def copies(chunk):
        rows = pl.ds(chunk * PAIR, PAIR)
        for which, (source, held) in enumerate(((x_hbm, x_held), (g_hbm, g_held))):
            yield pltpu.make_async_copy(source.at[rows, :], held.at[rows, :], sems.at[which, chunk])

    w_copy = pltpu.make_async_copy(w_hbm, w_held, w_sem)
    for chunk in range(chunks):
        for copy in copies(chunk):
            copy.start()
        if chunk == chunks // 2:
            w_copy.start()
    total[...] = jnp.zeros_like(total)
    for copy in tables:
        copy.wait()
    pair_up(system_ref, count_ref, pair_system, slot_block, slot_count)

    def copy_out(rows, lines, sem):
        return pltpu.make_async_copy(out_ref.at[rows, lines, :], out_hbm.at[rows, lines, :], out_sems.at[sem])

    sent = [copy_out(pl.ds(0, 128), pl.ds(64, 8), 0)]

    def pack_weights():
        w_copy.wait()
        own = lax.axis_index("dp")
        for half in range(2):
            pick = None
            for part in range(4):
                column = 256 * half + LANES * (part // 2)
                piece = w_held[:, column:column + LANES].astype(jnp.float32).reshape(64, TILE_ROWS, LANES)
                piece = piece[:, 8 * (part % 2):8 * (part % 2) + 8, :]
                pick = piece if pick is None else jnp.where(own == part, piece, pick)
            out_ref[64 * half:64 * half + 64, 64:72, :] = pick.astype(jnp.bfloat16)
        sent[0].start()

    done = arrived = 0
    for stage in STAGES:
        needed = min(done + stage + 1, chunks)
        for chunk in range(arrived, needed):
            for copy in copies(chunk):
                copy.wait()
        arrived = needed
        for pair in range(done, done + stage):
            mask, x_pair, g_pair = masked_pair((x_held, g_held), slot_block, slot_count, pair)
            system = pair_system[pair]
            x_real, x_imag = x_pair[:, :width] * mask, x_pair[:, width:] * mask
            g_real, g_imag = g_pair[:, :width], g_pair[:, width:]
            total[system, :, :width] += f32_dot(x_real + x_imag, g_real, FIRST)
            total[system, :, width:2 * width] += f32_dot(x_imag, g_imag - g_real, FIRST)
            total[system, :, 2 * width:] += f32_dot(x_real, g_real + g_imag, FIRST)
        done += stage
        if done == sum(STAGES[:-1]):
            pack_weights()

    for system in range(2):
        for half in range(2):
            for block in range(2):
                column = 256 * half + LANES * block
                shared = total[system, :, column:column + LANES]
                real = total[system, :, width + column:width + column + LANES] + shared
                imag = total[system, :, 2 * width + column:2 * width + column + LANES] - shared
                row = system * 32 + block * TILE_ROWS
                for plane, piece in enumerate((real, imag)):
                    at = 64 * half + 32 * plane
                    out_ref[at:at + 32, row:row + TILE_ROWS, :] = piece.astype(jnp.bfloat16).reshape(
                        32, TILE_ROWS, LANES
                    )
            sent.append(copy_out(pl.ds(64 * half, 64), pl.ds(32 * system, 32), len(sent)))
            sent[-1].start()
    for copy in sent:
        copy.wait()


def mix_kernel(factor, mix0, mix1, mix2, mix3, in_ref, out_ref):
    parts = (mix0, mix1, mix2, mix3)
    experts = mix0.shape[1]
    own = lax.axis_index("dp")
    at = [(own ^ j) * experts for j in range(4)]

    def merge(e, totals):
        pieces = [in_ref[d * experts + e, 64:72, :].astype(jnp.float32) for d in range(4)]
        return tuple(
            totals[s * 4 + d] + parts[s // 2][s % 2, e] * pieces[d] for s in range(8) for d in range(4)
        )

    zero = jnp.zeros((8, LANES), jnp.float32)
    merged = lax.fori_loop(0, experts, merge, (zero,) * 32, unroll=UNROLL)
    packed = [
        jnp.concatenate([merged[(2 * j + s) * 4 + i] for s in range(2) for i in range(4)], axis=0).astype(jnp.bfloat16)
        for j in range(4)
    ]

    def gather(e, totals):
        for j in range(4):
            out_ref[at[j] + e, 0:64, :] = packed[j]
        return tuple(totals[j] + in_ref[at[j] + e, 0:64, :].astype(jnp.float32) for j in range(4))

    zero = jnp.zeros((64, LANES), jnp.float32)
    grads = lax.fori_loop(0, experts, gather, (zero,) * 4, unroll=UNROLL)
    grads = [grad * factor for grad in grads]

    def combine(e, _):
        terms = [parts[j][s, e] * grads[j][32 * s:32 * s + 32] for j in range(4) for s in range(2)]
        result = sum(terms[1:], terms[0])
        for d in range(4):
            quarters = [result[8 * q:8 * q + 8] for q in (d, d ^ 2)]
            out_ref[d * experts + e, 64:80, :] = jnp.concatenate(quarters, axis=0).astype(jnp.bfloat16)
        return 0

    lax.fori_loop(0, experts, combine, 0, unroll=UNROLL)


def message_kernel(
    system_hbm, count_hbm, x_ref, g_ref, in_ref, out_hbm, back_hbm,
    out_held, back_held, weight, system_ref, count_ref, pair_system, slot_block, slot_count, table_sems, sems,
):
    width = x_ref.shape[1] // 2
    pairs = out_held.shape[0] // PAIR
    tables = table_copies(system_hbm, count_hbm, system_ref, count_ref, table_sems)
    for copy in tables:
        copy.start()

    for half in range(2):
        for block in range(2):
            column = 256 * half + LANES * block
            for system in range(2):
                row = 32 * system + block * TILE_ROWS
                piece = in_ref[64 * half:64 * half + 64, row:row + TILE_ROWS, :].reshape(2 * width, LANES)
                real, imag = piece[:width], piece[width:]
                weight[system, 0, :, column:column + LANES] = real
                weight[system, 1, :, column:column + LANES] = imag - real
                weight[system, 2, :, column:column + LANES] = real + imag

    for copy in tables:
        copy.wait()
    pair_up(system_ref, count_ref, pair_system, slot_block, slot_count)

    def copies(slot, b):
        for which, (held, target) in enumerate(((out_held, out_hbm), (back_held, back_hbm))):
            yield pltpu.make_async_copy(held.at[rows_of(slot), :], target.at[rows_of(b), :], sems.at[which, slot])

    for pair in range(pairs):
        rows = pl.ds(pair * PAIR, PAIR)
        system = pair_system[pair]
        mask, x_pair, g_pair = masked_pair((x_ref, g_ref), slot_block, slot_count, pair)
        x_real, x_imag = x_pair[:, :width] * mask, x_pair[:, width:] * mask
        shared = f32_dot(x_real + x_imag, weight[system, 0])
        out_held[rows, :width] = (shared - f32_dot(x_imag, weight[system, 2])).astype(jnp.bfloat16)
        out_held[rows, width:] = (shared + f32_dot(x_real, weight[system, 1])).astype(jnp.bfloat16)
        g_real, g_imag = g_pair[:, :width] * mask, g_pair[:, width:] * mask
        shared = f32_dot(g_real + g_imag, weight[system, 0], LAST)
        back_held[rows, :width] = (shared + f32_dot(g_imag, weight[system, 1], LAST)).astype(jnp.bfloat16)
        back_held[rows, width:] = (shared - f32_dot(g_real, weight[system, 2], LAST)).astype(jnp.bfloat16)
        for slot in (2 * pair, 2 * pair + 1):

            @pl.when(slot_count[slot] > 0)
            def _():
                for copy in copies(slot, slot_block[slot]):
                    copy.start()

    def finish(slot, _):
        @pl.when(slot_count[slot] > 0)
        def _():
            for copy in copies(slot, 0):
                copy.wait()

        return 0

    lax.fori_loop(0, 2 * pairs, finish, 0)


def expert_kernel(mine_ref, other_ref, out_hbm, held, sems):
    own = lax.axis_index("dp")
    odd, high = own % 2 == 1, own >= 2

    def copy_out(half, block):
        columns = pl.ds(256 * half + LANES * block, LANES)
        return pltpu.make_async_copy(held.at[:, columns], out_hbm.at[:, columns], sems.at[2 * half + block])

    for half in range(2):
        rows = slice(64 * half, 64 * half + 64)
        mine, other = mine_ref[rows, :, :].astype(jnp.float32), other_ref[rows, :, :].astype(jnp.float32)
        even_rows = jnp.where(odd, other, mine)
        odd_rows = jnp.where(odd, mine, other)
        for block in range(2):
            near = [jnp.where(high, q[:, 8:16], q[:, 0:8]) if block == 0 else jnp.where(high, q[:, 0:8], q[:, 8:16])
                    for q in (even_rows, odd_rows)]
            column = 256 * half + LANES * block
            held[:, column:column + LANES] = jnp.concatenate(near, axis=1).reshape(held.shape[0], LANES)
            copy_out(half, block).start()
    for half in range(2):
        for block in range(2):
            copy_out(half, block).wait()


def local(
    inputs, cotangent, expert_weights, fidelity_table, system_weights, fidelity, block_system, block_count
):
    edges, channels = inputs.shape
    width = channels // 2
    blocks = block_system.shape[0]
    pairs = blocks // 2 + 1
    axes = ("dp", "expert")
    devices = lax.axis_size("dp") * lax.axis_size("expert")
    experts = fidelity_table.shape[1]

    picked = jnp.zeros(system_weights.shape, jnp.float32)
    for f in range(fidelity_table.shape[0]):
        picked = jnp.where((fidelity == f)[:, None], fidelity_table[f][None, :], picked)
    mixing = picked * system_weights
    mixings = [mixing] + [
        lax.ppermute(mixing, "dp", [(i, i ^ j) for i in range(4)]) for j in range(1, 4)
    ]

    smem = pl.BlockSpec(memory_space=pltpu.SMEM)
    vmem = pl.BlockSpec(memory_space=pltpu.VMEM)
    hbm = pl.BlockSpec(memory_space=pltpu.HBM)
    params = pltpu.CompilerParams(vmem_limit_bytes=VMEM_LIMIT)
    held = pltpu.VMEM((pairs * PAIR, channels), jnp.bfloat16)
    whole = pltpu.VMEM((edges, channels), jnp.bfloat16)
    macs = edges * channels * channels
    tables = [pltpu.SMEM((size,), jnp.int32) for size in (blocks, blocks, pairs + 1, 2 * pairs + 2, 2 * pairs + 2)]

    def exchange(chunks):
        return lax.all_to_all(chunks, axes, split_axis=0, concat_axis=0, tiled=True)

    pinned = [
        pltpu.with_memory_space_constraint(array, pltpu.HBM)
        for array in (block_system, block_count, inputs, cotangent, expert_weights.reshape(channels, width))
    ]
    partial = pl.pallas_call(
        grad_kernel,
        out_shape=pltpu.HBM((devices, 72, LANES), jnp.bfloat16),
        in_specs=[hbm] * 5,
        out_specs=hbm,
        scratch_shapes=[
            whole,
            whole,
            pltpu.VMEM((devices, 72, LANES), jnp.bfloat16),
            pltpu.VMEM((2, width, 3 * width), jnp.float32),
            pltpu.VMEM((channels, width), jnp.bfloat16),
            *tables,
            pltpu.SemaphoreType.DMA((2,)),
            pltpu.SemaphoreType.DMA((2, edges // PAIR)),
            pltpu.SemaphoreType.DMA,
            pltpu.SemaphoreType.DMA((5,)),
        ],
        compiler_params=params,
        cost_estimate=pl.CostEstimate(flops=2 * macs, bytes_accessed=12 * 2**20, transcendentals=0),
        name="weight_gradients",
    )(*pinned)

    factor = experts / math.sqrt(edges * devices)
    arrived = exchange(partial)
    mixed = pl.pallas_call(
        functools.partial(mix_kernel, factor),
        out_shape=pltpu.VMEM((devices, 80, LANES), jnp.bfloat16),
        in_specs=[smem] * 4 + [vmem],
        out_specs=vmem,
        compiler_params=params,
        name="mixing",
    )(*mixings, pltpu.with_memory_space_constraint(arrived, pltpu.VMEM))

    received = exchange(mixed)
    halves = received[:, 64:80, :]
    halves = [halves, lax.ppermute(halves, "dp", [(i, i ^ 1) for i in range(4)])]
    messages, back = pl.pallas_call(
        message_kernel,
        out_shape=(
            jax.ShapeDtypeStruct((edges, channels), jnp.bfloat16),
            jax.ShapeDtypeStruct((edges, channels), jnp.bfloat16),
        ),
        in_specs=[hbm, hbm, vmem, vmem, vmem],
        out_specs=(hbm, hbm),
        scratch_shapes=[
            held,
            held,
            pltpu.VMEM((2, 3, width, width), jnp.bfloat16),
            *tables,
            pltpu.SemaphoreType.DMA((2,)),
            pltpu.SemaphoreType.DMA((2, 2 * pairs)),
        ],
        compiler_params=params,
        cost_estimate=pl.CostEstimate(flops=4 * macs, bytes_accessed=24 * 2**20, transcendentals=0),
        name="messages",
    )(*pinned[:2], pltpu.with_memory_space_constraint(inputs, pltpu.VMEM), pltpu.with_memory_space_constraint(cotangent, pltpu.VMEM), pltpu.with_memory_space_constraint(received, pltpu.VMEM))
    grad_experts = pl.pallas_call(
        expert_kernel,
        out_shape=jax.ShapeDtypeStruct((channels, width), jnp.float32),
        in_specs=[vmem] * 2,
        out_specs=hbm,
        scratch_shapes=[pltpu.VMEM((channels, width), jnp.float32), pltpu.SemaphoreType.DMA((4,))],
        compiler_params=params,
        name="expert_gradients",
    )(*[pltpu.with_memory_space_constraint(half, pltpu.VMEM) for half in halves])
    return (messages, back, grad_experts.reshape(expert_weights.shape))


def solution(mesh):
    in_specs = (
        P(("dp", "expert"), None),
        P(("dp", "expert"), None),
        P("expert", None, None, None),
        P(),
        P("dp", None),
        P("dp"),
        P(("dp", "expert")),
        P(("dp", "expert")),
    )
    out_specs = (
        P(("dp", "expert"), None),
        P(("dp", "expert"), None),
        P("expert", None, None, None),
    )
    return jax.shard_map(local, mesh=mesh, in_specs=in_specs, out_specs=out_specs, check_vma=False)
```

```python
import functools
import math

import jax
import jax.numpy as jnp
from jax import lax
from jax.experimental import pallas as pl
from jax.experimental.pallas import tpu as pltpu
from jax.sharding import PartitionSpec as P

BLOCK = 128
LANES = 128
TILE_ROWS = 16
PAIR = 2 * BLOCK
STAGES = (1, 2, 3, 3)
UNROLL = 4
VMEM_LIMIT = 32 * 1024 * 1024
FIRST = ((0,), (0,)), ((), ())
LAST = ((1,), (1,)), ((), ())


def f32_dot(a, b, dims=(((1,), (0,)), ((), ()))):
    return lax.dot_general(a, b, dims, preferred_element_type=jnp.float32)


def rows_of(index):
    return pl.ds(pl.multiple_of(index * BLOCK, BLOCK), BLOCK)


def pair_up(system_ref, count_ref, pair_system, slot_block, slot_count):
    blocks = system_ref.shape[0]
    pair = jnp.int32(0)
    waiting = [jnp.int32(-1), jnp.int32(-1)]
    for b in range(blocks):
        system = system_ref[b]
        mate = jnp.where(system == 0, waiting[0], waiting[1])
        paired = mate >= 0
        near = jnp.maximum(mate, 0)
        pair_system[pair] = system
        slot_block[2 * pair] = near
        slot_block[2 * pair + 1] = b
        slot_count[2 * pair] = count_ref[near]
        slot_count[2 * pair + 1] = count_ref[b]
        pair += paired.astype(jnp.int32)
        left = jnp.where(paired, -1, b)
        waiting = [jnp.where(system == s, left, waiting[s]) for s in range(2)]
    for system in range(2):
        alone = waiting[system] >= 0
        near = jnp.maximum(waiting[system], 0)
        pair_system[pair] = system
        slot_block[2 * pair] = near
        slot_block[2 * pair + 1] = near
        slot_count[2 * pair] = jnp.where(alone, count_ref[near], 0)
        slot_count[2 * pair + 1] = 0
        pair += alone.astype(jnp.int32)


def table_copies(system_hbm, count_hbm, system_ref, count_ref, sems):
    return [
        pltpu.make_async_copy(system_hbm, system_ref, sems.at[0]),
        pltpu.make_async_copy(count_hbm, count_ref, sems.at[1]),
    ]


def masked_pair(refs, slot_block, slot_count, pair):
    row = lax.broadcasted_iota(jnp.int32, (BLOCK, 1), 0)
    live = [(row < slot_count[2 * pair + i]).astype(jnp.float32) for i in range(2)]
    mask = jnp.concatenate(live, axis=0).astype(jnp.bfloat16)
    return mask, *[
        jnp.concatenate([ref[rows_of(slot_block[2 * pair + i]), :] for i in range(2)], axis=0) for ref in refs
    ]


def grad_kernel(
    system_hbm, count_hbm, x_hbm, g_hbm, w_hbm, out_hbm,
    x_held, g_held, out_ref, total, w_held, system_ref, count_ref, pair_system, slot_block, slot_count,
    table_sems, sems, w_sem, out_sems,
):
    width = x_hbm.shape[1] // 2
    chunks = x_hbm.shape[0] // PAIR
    tables = table_copies(system_hbm, count_hbm, system_ref, count_ref, table_sems)
    for copy in tables:
        copy.start()

    def copies(chunk):
        rows = pl.ds(chunk * PAIR, PAIR)
        for which, (source, held) in enumerate(((x_hbm, x_held), (g_hbm, g_held))):
            yield pltpu.make_async_copy(source.at[rows, :], held.at[rows, :], sems.at[which, chunk])

    w_copy = pltpu.make_async_copy(w_hbm, w_held, w_sem)
    for chunk in range(chunks):
        for copy in copies(chunk):
            copy.start()
        if chunk == chunks // 2:
            w_copy.start()
    total[...] = jnp.zeros_like(total)
    for copy in tables:
        copy.wait()
    pair_up(system_ref, count_ref, pair_system, slot_block, slot_count)

    def copy_out(rows, lines, sem):
        return pltpu.make_async_copy(out_ref.at[rows, lines, :], out_hbm.at[rows, lines, :], out_sems.at[sem])

    sent = [copy_out(pl.ds(0, 128), pl.ds(64, 8), 0)]

    def pack_weights():
        w_copy.wait()
        own = lax.axis_index("dp")
        for half in range(2):
            pick = None
            for part in range(4):
                column = 256 * half + LANES * (part // 2)
                piece = w_held[:, column:column + LANES].astype(jnp.float32).reshape(64, TILE_ROWS, LANES)
                piece = piece[:, 8 * (part % 2):8 * (part % 2) + 8, :]
                pick = piece if pick is None else jnp.where(own == part, piece, pick)
            out_ref[64 * half:64 * half + 64, 64:72, :] = pick.astype(jnp.bfloat16)
        sent[0].start()

    done = arrived = 0
    for stage in STAGES:
        needed = min(done + stage + 1, chunks)
        for chunk in range(arrived, needed):
            for copy in copies(chunk):
                copy.wait()
        arrived = needed
        for pair in range(done, done + stage):
            mask, x_pair, g_pair = masked_pair((x_held, g_held), slot_block, slot_count, pair)
            system = pair_system[pair]
            x_real, x_imag = x_pair[:, :width] * mask, x_pair[:, width:] * mask
            g_real, g_imag = g_pair[:, :width], g_pair[:, width:]
            total[system, :, :width] += f32_dot(x_real + x_imag, g_real, FIRST)
            total[system, :, width:2 * width] += f32_dot(x_imag, g_imag - g_real, FIRST)
            total[system, :, 2 * width:] += f32_dot(x_real, g_real + g_imag, FIRST)
        done += stage
        if done == sum(STAGES[:-1]):
            pack_weights()

    for system in range(2):
        for half in range(2):
            for block in range(2):
                column = 256 * half + LANES * block
                shared = total[system, :, column:column + LANES]
                real = total[system, :, width + column:width + column + LANES] + shared
                imag = total[system, :, 2 * width + column:2 * width + column + LANES] - shared
                row = system * 32 + block * TILE_ROWS
                for plane, piece in enumerate((real, imag)):
                    at = 64 * half + 32 * plane
                    out_ref[at:at + 32, row:row + TILE_ROWS, :] = piece.astype(jnp.bfloat16).reshape(
                        32, TILE_ROWS, LANES
                    )
            sent.append(copy_out(pl.ds(64 * half, 64), pl.ds(32 * system, 32), len(sent)))
            sent[-1].start()
    for copy in sent:
        copy.wait()


def mix_kernel(factor, mix0, mix1, mix2, mix3, in_ref, out_ref, held0, held1, held2, held3, sems):
    parts = (held0, held1, held2, held3)
    experts = mix0.shape[1]
    copies = [
        pltpu.make_async_copy(mix, part, sems.at[j])
        for j, (mix, part) in enumerate(zip((mix0, mix1, mix2, mix3), parts))
    ]
    for copy in copies:
        copy.start()
    own = lax.axis_index("dp")
    at = [(own ^ j) * experts for j in range(4)]

    def gather(e, totals):
        return tuple(totals[j] + in_ref[at[j] + e, 0:64, :].astype(jnp.float32) for j in range(4))

    zero = jnp.zeros((64, LANES), jnp.float32)
    grads = lax.fori_loop(0, experts, gather, (zero,) * 4, unroll=UNROLL)
    grads = [grad * factor for grad in grads]
    for copy in copies:
        copy.wait()

    def merge(e, totals):
        pieces = [in_ref[d * experts + e, 64:72, :].astype(jnp.float32) for d in range(4)]
        return tuple(
            totals[s * 4 + d] + parts[s // 2][s % 2, e] * pieces[d] for s in range(8) for d in range(4)
        )

    zero = jnp.zeros((8, LANES), jnp.float32)
    merged = lax.fori_loop(0, experts, merge, (zero,) * 32, unroll=UNROLL)
    packed = [
        jnp.concatenate([merged[(2 * j + s) * 4 + i] for s in range(2) for i in range(4)], axis=0).astype(jnp.bfloat16)
        for j in range(4)
    ]

    def spread(e, _):
        for j in range(4):
            out_ref[at[j] + e, 0:64, :] = packed[j]
        return 0

    lax.fori_loop(0, experts, spread, 0, unroll=UNROLL)

    def combine(e, _):
        terms = [parts[j][s, e] * grads[j][32 * s:32 * s + 32] for j in range(4) for s in range(2)]
        result = sum(terms[1:], terms[0])
        for d in range(4):
            quarters = [result[8 * q:8 * q + 8] for q in (d, d ^ 2)]
            out_ref[d * experts + e, 64:80, :] = jnp.concatenate(quarters, axis=0).astype(jnp.bfloat16)
        return 0

    lax.fori_loop(0, experts, combine, 0, unroll=UNROLL)


def sort_kernel(
    system_hbm, count_hbm, x_hbm, g_hbm, x_out, g_out,
    x_held, g_held, x_ref, g_ref, system_ref, count_ref, pair_system, slot_block, slot_count, table_sems, sems,
):
    copies = table_copies(system_hbm, count_hbm, system_ref, count_ref, table_sems)
    copies.append(pltpu.make_async_copy(x_hbm, x_held, sems.at[0]))
    copies.append(pltpu.make_async_copy(g_hbm, g_held, sems.at[1]))
    for copy in copies:
        copy.start()
    for copy in copies:
        copy.wait()
    pair_up(system_ref, count_ref, pair_system, slot_block, slot_count)
    for pair in range(x_ref.shape[0] // PAIR):
        rows = pl.ds(pair * PAIR, PAIR)
        mask, x_pair, g_pair = masked_pair((x_held, g_held), slot_block, slot_count, pair)
        x_ref[rows, :] = x_pair * mask
        g_ref[rows, :] = g_pair * mask
    copies = [
        pltpu.make_async_copy(x_ref, x_out, sems.at[0]),
        pltpu.make_async_copy(g_ref, g_out, sems.at[1]),
    ]
    for copy in copies:
        copy.start()
    for copy in copies:
        copy.wait()


def message_kernel(
    system_hbm, count_hbm, x_ref, g_ref, in_ref, out_hbm, back_hbm,
    out_held, back_held, weight, system_ref, count_ref, pair_system, slot_block, slot_count, table_sems, sems,
):
    width = x_ref.shape[1] // 2
    pairs = out_held.shape[0] // PAIR
    tables = table_copies(system_hbm, count_hbm, system_ref, count_ref, table_sems)
    for copy in tables:
        copy.start()

    for half in range(2):
        for block in range(2):
            column = 256 * half + LANES * block
            for system in range(2):
                row = 32 * system + block * TILE_ROWS
                piece = in_ref[64 * half:64 * half + 64, row:row + TILE_ROWS, :].reshape(2 * width, LANES)
                real, imag = piece[:width], piece[width:]
                weight[system, 0, :, column:column + LANES] = real
                weight[system, 1, :, column:column + LANES] = imag - real
                weight[system, 2, :, column:column + LANES] = real + imag

    for copy in tables:
        copy.wait()
    pair_up(system_ref, count_ref, pair_system, slot_block, slot_count)

    def copies(slot, b):
        for which, (held, target) in enumerate(((out_held, out_hbm), (back_held, back_hbm))):
            yield pltpu.make_async_copy(held.at[rows_of(slot), :], target.at[rows_of(b), :], sems.at[which, slot])

    for pair in range(pairs):
        rows = pl.ds(pair * PAIR, PAIR)
        system = pair_system[pair]
        x_real, x_imag = x_ref[rows, :width], x_ref[rows, width:]
        shared = f32_dot(x_real + x_imag, weight[system, 0])
        out_held[rows, :width] = (shared - f32_dot(x_imag, weight[system, 2])).astype(jnp.bfloat16)
        out_held[rows, width:] = (shared + f32_dot(x_real, weight[system, 1])).astype(jnp.bfloat16)
        g_real, g_imag = g_ref[rows, :width], g_ref[rows, width:]
        shared = f32_dot(g_real + g_imag, weight[system, 0], LAST)
        back_held[rows, :width] = (shared + f32_dot(g_imag, weight[system, 1], LAST)).astype(jnp.bfloat16)
        back_held[rows, width:] = (shared - f32_dot(g_real, weight[system, 2], LAST)).astype(jnp.bfloat16)
        for slot in (2 * pair, 2 * pair + 1):

            @pl.when(slot_count[slot] > 0)
            def _():
                for copy in copies(slot, slot_block[slot]):
                    copy.start()

    def finish(slot, _):
        @pl.when(slot_count[slot] > 0)
        def _():
            for copy in copies(slot, 0):
                copy.wait()

        return 0

    lax.fori_loop(0, 2 * pairs, finish, 0)


def expert_kernel(mine_ref, other_ref, out_hbm, held, sems):
    own = lax.axis_index("dp")
    odd, high = own % 2 == 1, own >= 2

    def copy_out(half, block):
        columns = pl.ds(256 * half + LANES * block, LANES)
        return pltpu.make_async_copy(held.at[:, columns], out_hbm.at[:, columns], sems.at[2 * half + block])

    for half in range(2):
        rows = slice(64 * half, 64 * half + 64)
        mine, other = mine_ref[rows, :, :].astype(jnp.float32), other_ref[rows, :, :].astype(jnp.float32)
        even_rows = jnp.where(odd, other, mine)
        odd_rows = jnp.where(odd, mine, other)
        for block in range(2):
            near = [jnp.where(high, q[:, 8:16], q[:, 0:8]) if block == 0 else jnp.where(high, q[:, 0:8], q[:, 8:16])
                    for q in (even_rows, odd_rows)]
            column = 256 * half + LANES * block
            held[:, column:column + LANES] = jnp.concatenate(near, axis=1).reshape(held.shape[0], LANES)
            copy_out(half, block).start()
    for half in range(2):
        for block in range(2):
            copy_out(half, block).wait()


def local(
    inputs, cotangent, expert_weights, fidelity_table, system_weights, fidelity, block_system, block_count
):
    edges, channels = inputs.shape
    width = channels // 2
    blocks = block_system.shape[0]
    pairs = blocks // 2 + 1
    axes = ("dp", "expert")
    devices = lax.axis_size("dp") * lax.axis_size("expert")
    experts = fidelity_table.shape[1]

    picked = jnp.zeros(system_weights.shape, jnp.float32)
    for f in range(fidelity_table.shape[0]):
        picked = jnp.where((fidelity == f)[:, None], fidelity_table[f][None, :], picked)
    mixing = picked * system_weights
    mixings = [mixing] + [
        lax.ppermute(mixing, "dp", [(i, i ^ j) for i in range(4)]) for j in range(1, 4)
    ]

    vmem = pl.BlockSpec(memory_space=pltpu.VMEM)
    hbm = pl.BlockSpec(memory_space=pltpu.HBM)
    params = pltpu.CompilerParams(vmem_limit_bytes=VMEM_LIMIT)
    held = pltpu.VMEM((pairs * PAIR, channels), jnp.bfloat16)
    whole = pltpu.VMEM((edges, channels), jnp.bfloat16)
    macs = edges * channels * channels
    tables = [pltpu.SMEM((size,), jnp.int32) for size in (blocks, blocks, pairs + 1, 2 * pairs + 2, 2 * pairs + 2)]

    def exchange(chunks):
        return lax.all_to_all(chunks, axes, split_axis=0, concat_axis=0, tiled=True)

    pinned = [
        pltpu.with_memory_space_constraint(array, pltpu.HBM)
        for array in (block_system, block_count, inputs, cotangent, expert_weights.reshape(channels, width))
    ]
    partial = pl.pallas_call(
        grad_kernel,
        out_shape=pltpu.HBM((devices, 72, LANES), jnp.bfloat16),
        in_specs=[hbm] * 5,
        out_specs=hbm,
        scratch_shapes=[
            whole,
            whole,
            pltpu.VMEM((devices, 72, LANES), jnp.bfloat16),
            pltpu.VMEM((2, width, 3 * width), jnp.float32),
            pltpu.VMEM((channels, width), jnp.bfloat16),
            *tables,
            pltpu.SemaphoreType.DMA((2,)),
            pltpu.SemaphoreType.DMA((2, edges // PAIR)),
            pltpu.SemaphoreType.DMA,
            pltpu.SemaphoreType.DMA((5,)),
        ],
        compiler_params=params,
        cost_estimate=pl.CostEstimate(flops=2 * macs, bytes_accessed=12 * 2**20, transcendentals=0),
        name="weight_gradients",
    )(*pinned)

    x_sorted, g_sorted = pl.pallas_call(
        sort_kernel,
        out_shape=(jax.ShapeDtypeStruct((pairs * PAIR, channels), jnp.bfloat16),) * 2,
        in_specs=[hbm] * 4,
        out_specs=(hbm, hbm),
        scratch_shapes=[
            whole,
            whole,
            held,
            held,
            *tables,
            pltpu.SemaphoreType.DMA((2,)),
            pltpu.SemaphoreType.DMA((2,)),
        ],
        compiler_params=params,
        cost_estimate=pl.CostEstimate(flops=2**20, bytes_accessed=20 * 2**20, transcendentals=0),
        name="sort_edges",
    )(*pinned[:4])

    mixings[0], x_sorted, g_sorted = lax.optimization_barrier((mixings[0], x_sorted, g_sorted))

    factor = experts / math.sqrt(edges * devices)
    arrived = exchange(partial)
    mixed = pl.pallas_call(
        functools.partial(mix_kernel, factor),
        out_shape=pltpu.VMEM((devices, 80, LANES), jnp.bfloat16),
        in_specs=[vmem] * 5,
        out_specs=vmem,
        scratch_shapes=[pltpu.SMEM((2, experts), jnp.float32)] * 4 + [pltpu.SemaphoreType.DMA((4,))],
        compiler_params=params,
        name="mixing",
    )(*[pltpu.with_memory_space_constraint(mixing, pltpu.VMEM) for mixing in mixings], pltpu.with_memory_space_constraint(arrived, pltpu.VMEM))

    received = exchange(mixed)
    halves = received[:, 64:80, :]
    halves = [halves, lax.ppermute(halves, "dp", [(i, i ^ 1) for i in range(4)])]
    messages, back = pl.pallas_call(
        message_kernel,
        out_shape=(
            jax.ShapeDtypeStruct((edges, channels), jnp.bfloat16),
            jax.ShapeDtypeStruct((edges, channels), jnp.bfloat16),
        ),
        in_specs=[hbm, hbm, vmem, vmem, vmem],
        out_specs=(hbm, hbm),
        scratch_shapes=[
            held,
            held,
            pltpu.VMEM((2, 3, width, width), jnp.bfloat16),
            *tables,
            pltpu.SemaphoreType.DMA((2,)),
            pltpu.SemaphoreType.DMA((2, 2 * pairs)),
        ],
        compiler_params=params,
        cost_estimate=pl.CostEstimate(flops=4 * macs, bytes_accessed=24 * 2**20, transcendentals=0),
        name="messages",
    )(*pinned[:2], pltpu.with_memory_space_constraint(x_sorted, pltpu.VMEM), pltpu.with_memory_space_constraint(g_sorted, pltpu.VMEM), pltpu.with_memory_space_constraint(received, pltpu.VMEM))
    grad_experts = pl.pallas_call(
        expert_kernel,
        out_shape=jax.ShapeDtypeStruct((channels, width), jnp.float32),
        in_specs=[vmem] * 2,
        out_specs=hbm,
        scratch_shapes=[pltpu.VMEM((channels, width), jnp.float32), pltpu.SemaphoreType.DMA((4,))],
        compiler_params=params,
        name="expert_gradients",
    )(*[pltpu.with_memory_space_constraint(half, pltpu.VMEM) for half in halves])
    return (messages, back, grad_experts.reshape(expert_weights.shape))


def solution(mesh):
    in_specs = (
        P(("dp", "expert"), None),
        P(("dp", "expert"), None),
        P("expert", None, None, None),
        P(),
        P("dp", None),
        P("dp"),
        P(("dp", "expert")),
        P(("dp", "expert")),
    )
    out_specs = (
        P(("dp", "expert"), None),
        P(("dp", "expert"), None),
        P("expert", None, None, None),
    )
    return jax.shard_map(local, mesh=mesh, in_specs=in_specs, out_specs=out_specs, check_vma=False)
```

```python
import functools
import math

import jax
import jax.numpy as jnp
from jax import lax
from jax.experimental import pallas as pl
from jax.experimental.pallas import tpu as pltpu
from jax.sharding import PartitionSpec as P

BLOCK = 128
LANES = 128
TILE_ROWS = 16
PAIR = 2 * BLOCK
STAGES = (1, 2, 3, 3)
UNROLL = 4
VMEM_LIMIT = 32 * 1024 * 1024
FIRST = ((0,), (0,)), ((), ())
LAST = ((1,), (1,)), ((), ())


def f32_dot(a, b, dims=(((1,), (0,)), ((), ()))):
    return lax.dot_general(a, b, dims, preferred_element_type=jnp.float32)


def rows_of(index):
    return pl.ds(pl.multiple_of(index * BLOCK, BLOCK), BLOCK)


def pair_up(system_ref, count_ref, pair_system, slot_block, slot_count):
    blocks = system_ref.shape[0]
    pair = jnp.int32(0)
    waiting = [jnp.int32(-1), jnp.int32(-1)]
    for b in range(blocks):
        system = system_ref[b]
        mate = jnp.where(system == 0, waiting[0], waiting[1])
        paired = mate >= 0
        near = jnp.maximum(mate, 0)
        pair_system[pair] = system
        slot_block[2 * pair] = near
        slot_block[2 * pair + 1] = b
        slot_count[2 * pair] = count_ref[near]
        slot_count[2 * pair + 1] = count_ref[b]
        pair += paired.astype(jnp.int32)
        left = jnp.where(paired, -1, b)
        waiting = [jnp.where(system == s, left, waiting[s]) for s in range(2)]
    for system in range(2):
        alone = waiting[system] >= 0
        near = jnp.maximum(waiting[system], 0)
        pair_system[pair] = system
        slot_block[2 * pair] = near
        slot_block[2 * pair + 1] = near
        slot_count[2 * pair] = jnp.where(alone, count_ref[near], 0)
        slot_count[2 * pair + 1] = 0
        pair += alone.astype(jnp.int32)


def table_copies(system_hbm, count_hbm, system_ref, count_ref, sems):
    return [
        pltpu.make_async_copy(system_hbm, system_ref, sems.at[0]),
        pltpu.make_async_copy(count_hbm, count_ref, sems.at[1]),
    ]


def masked_pair(refs, slot_block, slot_count, pair):
    row = lax.broadcasted_iota(jnp.int32, (BLOCK, 1), 0)
    live = [(row < slot_count[2 * pair + i]).astype(jnp.float32) for i in range(2)]
    mask = jnp.concatenate(live, axis=0).astype(jnp.bfloat16)
    return mask, *[
        jnp.concatenate([ref[rows_of(slot_block[2 * pair + i]), :] for i in range(2)], axis=0) for ref in refs
    ]


def grad_kernel(
    system_hbm, count_hbm, x_hbm, g_hbm, w_hbm, out_hbm,
    x_held, g_held, out_ref, total, w_held, system_ref, count_ref, pair_system, slot_block, slot_count,
    table_sems, sems, w_sem, out_sems,
):
    width = x_hbm.shape[1] // 2
    chunks = x_hbm.shape[0] // PAIR
    tables = table_copies(system_hbm, count_hbm, system_ref, count_ref, table_sems)
    for copy in tables:
        copy.start()

    def copies(chunk):
        rows = pl.ds(chunk * PAIR, PAIR)
        for which, (source, held) in enumerate(((x_hbm, x_held), (g_hbm, g_held))):
            yield pltpu.make_async_copy(source.at[rows, :], held.at[rows, :], sems.at[which, chunk])

    w_copy = pltpu.make_async_copy(w_hbm, w_held, w_sem)
    w_copy.start()
    for chunk in range(chunks):
        for copy in copies(chunk):
            copy.start()
    total[...] = jnp.zeros_like(total)
    for copy in tables:
        copy.wait()
    pair_up(system_ref, count_ref, pair_system, slot_block, slot_count)

    def copy_out(rows, lines, sem):
        return pltpu.make_async_copy(out_ref.at[rows, lines, :], out_hbm.at[rows, lines, :], out_sems.at[sem])

    sent = [copy_out(pl.ds(0, 128), pl.ds(64, 8), 0)]

    def pack_weights():
        w_copy.wait()
        own = lax.axis_index("dp")
        for half in range(2):
            pick = None
            for part in range(4):
                column = 256 * half + LANES * (part // 2)
                piece = w_held[:, column:column + LANES].astype(jnp.float32).reshape(64, TILE_ROWS, LANES)
                piece = piece[:, 8 * (part % 2):8 * (part % 2) + 8, :]
                pick = piece if pick is None else jnp.where(own == part, piece, pick)
            out_ref[64 * half:64 * half + 64, 64:72, :] = pick.astype(jnp.bfloat16)
        sent[0].start()

    pack_weights()
    done = arrived = 0
    for stage in STAGES:
        needed = min(done + stage + 1, chunks)
        for chunk in range(arrived, needed):
            for copy in copies(chunk):
                copy.wait()
        arrived = needed
        for pair in range(done, done + stage):
            mask, x_pair, g_pair = masked_pair((x_held, g_held), slot_block, slot_count, pair)
            system = pair_system[pair]
            x_real, x_imag = x_pair[:, :width] * mask, x_pair[:, width:] * mask
            g_real, g_imag = g_pair[:, :width], g_pair[:, width:]
            total[system, :, :width] += f32_dot(x_real + x_imag, g_real, FIRST)
            total[system, :, width:2 * width] += f32_dot(x_imag, g_imag - g_real, FIRST)
            total[system, :, 2 * width:] += f32_dot(x_real, g_real + g_imag, FIRST)
        done += stage

    for system in range(2):
        for half in range(2):
            for block in range(2):
                column = 256 * half + LANES * block
                shared = total[system, :, column:column + LANES]
                real = total[system, :, width + column:width + column + LANES] + shared
                imag = total[system, :, 2 * width + column:2 * width + column + LANES] - shared
                row = system * 32 + block * TILE_ROWS
                for plane, piece in enumerate((real, imag)):
                    at = 64 * half + 32 * plane
                    out_ref[at:at + 32, row:row + TILE_ROWS, :] = piece.astype(jnp.bfloat16).reshape(
                        32, TILE_ROWS, LANES
                    )
            sent.append(copy_out(pl.ds(64 * half, 64), pl.ds(32 * system, 32), len(sent)))
            sent[-1].start()
    for copy in sent:
        copy.wait()


def mix_kernel(factor, mix0, mix1, mix2, mix3, in_ref, out_ref, held0, held1, held2, held3, sems):
    parts = (held0, held1, held2, held3)
    experts = mix0.shape[1]
    copies = [
        pltpu.make_async_copy(mix, part, sems.at[j])
        for j, (mix, part) in enumerate(zip((mix0, mix1, mix2, mix3), parts))
    ]
    for copy in copies:
        copy.start()
    own = lax.axis_index("dp")
    at = [(own ^ j) * experts for j in range(4)]

    def gather(e, totals):
        return tuple(totals[j] + in_ref[at[j] + e, 0:64, :].astype(jnp.float32) for j in range(4))

    zero = jnp.zeros((64, LANES), jnp.float32)
    grads = lax.fori_loop(0, experts, gather, (zero,) * 4, unroll=UNROLL)
    grads = [grad * factor for grad in grads]
    for copy in copies:
        copy.wait()

    def merge(e, totals):
        pieces = [in_ref[d * experts + e, 64:72, :].astype(jnp.float32) for d in range(4)]
        return tuple(
            totals[s * 4 + d] + parts[s // 2][s % 2, e] * pieces[d] for s in range(8) for d in range(4)
        )

    zero = jnp.zeros((8, LANES), jnp.float32)
    merged = lax.fori_loop(0, experts, merge, (zero,) * 32, unroll=UNROLL)
    packed = [
        jnp.concatenate([merged[(2 * j + s) * 4 + i] for s in range(2) for i in range(4)], axis=0).astype(jnp.bfloat16)
        for j in range(4)
    ]

    def spread(e, _):
        for j in range(4):
            out_ref[at[j] + e, 0:64, :] = packed[j]
        return 0

    lax.fori_loop(0, experts, spread, 0, unroll=UNROLL)

    def combine(e, _):
        terms = [parts[j][s, e] * grads[j][32 * s:32 * s + 32] for j in range(4) for s in range(2)]
        result = sum(terms[1:], terms[0])
        for d in range(4):
            quarters = [result[8 * q:8 * q + 8] for q in (d, d ^ 2)]
            out_ref[d * experts + e, 64:80, :] = jnp.concatenate(quarters, axis=0).astype(jnp.bfloat16)
        return 0

    lax.fori_loop(0, experts, combine, 0, unroll=UNROLL)


def message_kernel(
    system_hbm, count_hbm, x_ref, g_ref, in_ref, out_hbm, back_hbm,
    out_held, back_held, weight, system_ref, count_ref, pair_system, slot_block, slot_count, table_sems, sems,
):
    width = x_ref.shape[1] // 2
    pairs = out_held.shape[0] // PAIR
    tables = table_copies(system_hbm, count_hbm, system_ref, count_ref, table_sems)
    for copy in tables:
        copy.start()

    for half in range(2):
        for block in range(2):
            column = 256 * half + LANES * block
            for system in range(2):
                row = 32 * system + block * TILE_ROWS
                piece = in_ref[64 * half:64 * half + 64, row:row + TILE_ROWS, :].reshape(2 * width, LANES)
                real, imag = piece[:width], piece[width:]
                weight[system, 0, :, column:column + LANES] = real
                weight[system, 1, :, column:column + LANES] = imag - real
                weight[system, 2, :, column:column + LANES] = real + imag

    for copy in tables:
        copy.wait()
    pair_up(system_ref, count_ref, pair_system, slot_block, slot_count)

    def copies(slot, b):
        for which, (held, target) in enumerate(((out_held, out_hbm), (back_held, back_hbm))):
            yield pltpu.make_async_copy(held.at[rows_of(slot), :], target.at[rows_of(b), :], sems.at[which, slot])

    for pair in range(pairs):
        rows = pl.ds(pair * PAIR, PAIR)
        system = pair_system[pair]
        mask, x_pair, g_pair = masked_pair((x_ref, g_ref), slot_block, slot_count, pair)
        x_real, x_imag = x_pair[:, :width] * mask, x_pair[:, width:] * mask
        shared = f32_dot(x_real + x_imag, weight[system, 0])
        out_held[rows, :width] = (shared - f32_dot(x_imag, weight[system, 2])).astype(jnp.bfloat16)
        out_held[rows, width:] = (shared + f32_dot(x_real, weight[system, 1])).astype(jnp.bfloat16)
        g_real, g_imag = g_pair[:, :width] * mask, g_pair[:, width:] * mask
        shared = f32_dot(g_real + g_imag, weight[system, 0], LAST)
        back_held[rows, :width] = (shared + f32_dot(g_imag, weight[system, 1], LAST)).astype(jnp.bfloat16)
        back_held[rows, width:] = (shared - f32_dot(g_real, weight[system, 2], LAST)).astype(jnp.bfloat16)
        for slot in (2 * pair, 2 * pair + 1):

            @pl.when(slot_count[slot] > 0)
            def _():
                for copy in copies(slot, slot_block[slot]):
                    copy.start()

    def finish(slot, _):
        @pl.when(slot_count[slot] > 0)
        def _():
            for copy in copies(slot, 0):
                copy.wait()

        return 0

    lax.fori_loop(0, 2 * pairs, finish, 0)


def expert_kernel(mine_ref, other_ref, out_hbm, held, sems):
    own = lax.axis_index("dp")
    odd, high = own % 2 == 1, own >= 2

    def copy_out(half, block):
        columns = pl.ds(256 * half + LANES * block, LANES)
        return pltpu.make_async_copy(held.at[:, columns], out_hbm.at[:, columns], sems.at[2 * half + block])

    for half in range(2):
        rows = slice(64 * half, 64 * half + 64)
        mine, other = mine_ref[rows, :, :].astype(jnp.float32), other_ref[rows, :, :].astype(jnp.float32)
        even_rows = jnp.where(odd, other, mine)
        odd_rows = jnp.where(odd, mine, other)
        for block in range(2):
            near = [jnp.where(high, q[:, 8:16], q[:, 0:8]) if block == 0 else jnp.where(high, q[:, 0:8], q[:, 8:16])
                    for q in (even_rows, odd_rows)]
            column = 256 * half + LANES * block
            held[:, column:column + LANES] = jnp.concatenate(near, axis=1).reshape(held.shape[0], LANES)
            copy_out(half, block).start()
    for half in range(2):
        for block in range(2):
            copy_out(half, block).wait()


def local(
    inputs, cotangent, expert_weights, fidelity_table, system_weights, fidelity, block_system, block_count
):
    edges, channels = inputs.shape
    width = channels // 2
    blocks = block_system.shape[0]
    pairs = blocks // 2 + 1
    axes = ("dp", "expert")
    devices = lax.axis_size("dp") * lax.axis_size("expert")
    experts = fidelity_table.shape[1]

    picked = jnp.zeros(system_weights.shape, jnp.float32)
    for f in range(fidelity_table.shape[0]):
        picked = jnp.where((fidelity == f)[:, None], fidelity_table[f][None, :], picked)
    mixing = picked * system_weights
    mixings = [mixing] + [
        lax.ppermute(mixing, "dp", [(i, i ^ j) for i in range(4)]) for j in range(1, 4)
    ]

    vmem = pl.BlockSpec(memory_space=pltpu.VMEM)
    hbm = pl.BlockSpec(memory_space=pltpu.HBM)
    params = pltpu.CompilerParams(vmem_limit_bytes=VMEM_LIMIT)
    held = pltpu.VMEM((pairs * PAIR, channels), jnp.bfloat16)
    whole = pltpu.VMEM((edges, channels), jnp.bfloat16)
    macs = edges * channels * channels
    tables = [pltpu.SMEM((size,), jnp.int32) for size in (blocks, blocks, pairs + 1, 2 * pairs + 2, 2 * pairs + 2)]

    def exchange(chunks):
        return lax.all_to_all(chunks, axes, split_axis=0, concat_axis=0, tiled=True)

    pinned = [
        pltpu.with_memory_space_constraint(array, pltpu.HBM)
        for array in (block_system, block_count, inputs, cotangent, expert_weights.reshape(channels, width))
    ]
    partial = pl.pallas_call(
        grad_kernel,
        out_shape=pltpu.HBM((devices, 72, LANES), jnp.bfloat16),
        in_specs=[hbm] * 5,
        out_specs=hbm,
        scratch_shapes=[
            whole,
            whole,
            pltpu.VMEM((devices, 72, LANES), jnp.bfloat16),
            pltpu.VMEM((2, width, 3 * width), jnp.float32),
            pltpu.VMEM((channels, width), jnp.bfloat16),
            *tables,
            pltpu.SemaphoreType.DMA((2,)),
            pltpu.SemaphoreType.DMA((2, edges // PAIR)),
            pltpu.SemaphoreType.DMA,
            pltpu.SemaphoreType.DMA((5,)),
        ],
        compiler_params=params,
        cost_estimate=pl.CostEstimate(flops=2 * macs, bytes_accessed=12 * 2**20, transcendentals=0),
        name="weight_gradients",
    )(*pinned)

    factor = experts / math.sqrt(edges * devices)
    arrived = exchange(partial)
    mixed = pl.pallas_call(
        functools.partial(mix_kernel, factor),
        out_shape=pltpu.VMEM((devices, 80, LANES), jnp.bfloat16),
        in_specs=[vmem] * 5,
        out_specs=vmem,
        scratch_shapes=[pltpu.SMEM((2, experts), jnp.float32)] * 4 + [pltpu.SemaphoreType.DMA((4,))],
        compiler_params=params,
        name="mixing",
    )(*[pltpu.with_memory_space_constraint(mixing, pltpu.VMEM) for mixing in mixings], pltpu.with_memory_space_constraint(arrived, pltpu.VMEM))

    received = exchange(mixed)
    halves = received[:, 64:80, :]
    halves = [halves, lax.ppermute(halves, "dp", [(i, i ^ 1) for i in range(4)])]
    messages, back = pl.pallas_call(
        message_kernel,
        out_shape=(
            jax.ShapeDtypeStruct((edges, channels), jnp.bfloat16),
            jax.ShapeDtypeStruct((edges, channels), jnp.bfloat16),
        ),
        in_specs=[hbm, hbm, vmem, vmem, vmem],
        out_specs=(hbm, hbm),
        scratch_shapes=[
            held,
            held,
            pltpu.VMEM((2, 3, width, width), jnp.bfloat16),
            *tables,
            pltpu.SemaphoreType.DMA((2,)),
            pltpu.SemaphoreType.DMA((2, 2 * pairs)),
        ],
        compiler_params=params,
        cost_estimate=pl.CostEstimate(flops=4 * macs, bytes_accessed=24 * 2**20, transcendentals=0),
        name="messages",
    )(*pinned[:2], pltpu.with_memory_space_constraint(inputs, pltpu.VMEM), pltpu.with_memory_space_constraint(cotangent, pltpu.VMEM), pltpu.with_memory_space_constraint(received, pltpu.VMEM))
    grad_experts = pl.pallas_call(
        expert_kernel,
        out_shape=jax.ShapeDtypeStruct((channels, width), jnp.float32),
        in_specs=[vmem] * 2,
        out_specs=hbm,
        scratch_shapes=[pltpu.VMEM((channels, width), jnp.float32), pltpu.SemaphoreType.DMA((4,))],
        compiler_params=params,
        name="expert_gradients",
    )(*[pltpu.with_memory_space_constraint(half, pltpu.VMEM) for half in halves])
    return (messages, back, grad_experts.reshape(expert_weights.shape))


def solution(mesh):
    in_specs = (
        P(("dp", "expert"), None),
        P(("dp", "expert"), None),
        P("expert", None, None, None),
        P(),
        P("dp", None),
        P("dp"),
        P(("dp", "expert")),
        P(("dp", "expert")),
    )
    out_specs = (
        P(("dp", "expert"), None),
        P(("dp", "expert"), None),
        P("expert", None, None, None),
    )
    return jax.shard_map(local, mesh=mesh, in_specs=in_specs, out_specs=out_specs, check_vma=False)
```
